512 devices in a mesh: ctx: 16 (over z_lo, x), tp: 16 (over z_hi, y), dp: 2 (over core).
Axes of the slice: x: 4, y: 8, z: 8 (z_hi: 2, z_lo: 4; z = z_hi * 4 + z_lo), core: 2. Of those that a mesh axis runs over, the one named last changes fastest.
Arguments:
- image_tokens: bfloat16 [16384, 3072], P(('dp', 'ctx', 'tp')), parts along dimension 0, may hold values from -50 to 50
- text_tokens: bfloat16 [512, 3072], P(('dp', 'tp')), parts along dimension 0, may hold values from -50 to 50
- image_modulation: float32 [6, 3072], P('dp'), parts along dimension 0, may hold values from -4 to 4
- text_modulation: float32 [6, 3072], P('dp'), parts along dimension 0, may hold values from -4 to 4
- image_projection: bfloat16 [3072, 6144], P(None, 'tp'), may hold values from -0.109375 to 0.109375
- text_projection: bfloat16 [3072, 6144], P('ctx', 'tp'), may hold values from -0.109375 to 0.109375
- image_merge: bfloat16 [2048, 3072], P('tp'), may hold values from -0.59765625 to 0.59765625
- text_merge: bfloat16 [2048, 3072], P('tp', 'ctx'), may hold values from -0.59765625 to 0.59765625
- norm_gains: float32 [4, 128], replicated, may hold values from 0.5 to 16
Outputs:
- image_update: bfloat16 [16384, 3072], P(('dp', 'ctx', 'tp')), parts along dimension 0
- text_update: bfloat16 [512, 3072], P(('dp', 'tp'), 'ctx'), parts along dimension 0
The draws below stay inside these ranges and needn't reach their ends.
There are 2 independent parts, one for each index of `dp`. The reference program is written for one: setup_inputs(seed, part) draws one part's arguments, and reference() takes and returns one part's arrays. A program takes and returns all parts, laid end to end along the dimension named above; an argument that names none is the same for every part. Nothing has to cross between parts.
All inputs are finite; a program needn't handle non-finite values.
Results may differ from the reference program's by a relative error of at most 0.025.
The reference program's roundings to bfloat16 on the way count: a program that leaves them out, or rounds other values in their place, can miss the bound.
Values may be sent and summed in bfloat16 or wider, within the bound.
A program may use at most 64 MiB of HBM per device.

```python
import jax
import jax.numpy as jnp
from jax import lax

D = 3072
HEADS = 16
HEAD_DIM = 128
TEXT = 256
IMAGE = 8192
N_TP = 16


def spread_scales(key, count, width):
    row_key, column_key = jax.random.split(key)
    row_scale = jnp.exp(jax.random.uniform(row_key, (count, 1), jnp.float32, -1.15, 1.15))
    column_scale = jnp.exp(jax.random.uniform(column_key, (1, width), jnp.float32, -1.15, 1.15))
    return row_scale * column_scale


def scaled_field(key, count, width):
    base_key, scale_key = jax.random.split(key, 2)
    base = jnp.clip(jax.random.normal(base_key, (count, width), jnp.float32), -5.0, 5.0)
    return base * spread_scales(scale_key, count, width)


def draw_image_tokens(key, part):
    key = jax.random.fold_in(key, 11)
    return scaled_field(key, IMAGE, D).astype(jnp.bfloat16)


def draw_text_tokens(key, part):
    key = jax.random.fold_in(key, 13)
    return scaled_field(key, TEXT, D).astype(jnp.bfloat16)


def draw_norm_gains(key, part):
    key = jax.random.fold_in(key, 17)
    gain_key = jax.random.fold_in(key, 0)
    gains = jnp.exp(jax.random.uniform(gain_key, (4, HEAD_DIM), jnp.float32, -0.69, 0.69))
    return gains


def levels(key, dims, pieces, low, largest):
    factor_of, own = 1.0, jax.random.fold_in(key, 6)
    for dim, shards_of in pieces:
        heights = jnp.exp(jax.random.uniform(jax.random.fold_in(own, dim), (shards_of,), jnp.float32, low / len(pieces), largest / len(pieces)))
        factor_of = factor_of * jnp.repeat(heights, dims[dim] // shards_of).reshape([-1 if axis == dim else 1 for axis in range(len(dims))])
    return factor_of


def bell_draw(own_key, shape, scale, bound, shards=(), held_as=jnp.bfloat16):
    values = scale * jax.random.normal(own_key, shape, jnp.float32)
    if shards:
        values = values * levels(own_key, shape, shards, -0.22, 0.18)
    return jnp.clip(values, -bound, bound).astype(held_as)


def setup_inputs(seed: int = 0, part: int = 0) -> dict:
    key_list = jax.random.split(jax.random.key(seed), 10)
    part_keys = jax.random.split(jax.random.fold_in(key_list[9], part), 10)
    image_tokens = draw_image_tokens(jax.random.fold_in(jax.random.fold_in(key_list[9], part), 71), part)
    text_tokens = draw_text_tokens(jax.random.fold_in(jax.random.fold_in(key_list[9], part), 71), part)
    image_modulation = bell_draw(part_keys[2], (3, D), 1.0, 4.0, (), jnp.float32)
    text_modulation = bell_draw(part_keys[3], (3, D), 1.0, 4.0, (), jnp.float32)
    image_projection = bell_draw(key_list[4], (D, 3 * HEADS * HEAD_DIM), D ** -0.5, 0.109375, ((1, 16),))
    text_projection = bell_draw(key_list[5], (D, 3 * HEADS * HEAD_DIM), D ** -0.5, 0.109375, ((0, 16), (1, 16)))
    image_merge = bell_draw(key_list[6], (HEADS * HEAD_DIM, D), 0.1, 0.59765625, ((0, 16),))
    text_merge = bell_draw(key_list[7], (HEADS * HEAD_DIM, D), 0.1, 0.59765625, ((0, 16), (1, 16)))
    norm_gains = draw_norm_gains(jax.random.fold_in(key_list[9], 71), part)
    return dict(image_tokens=image_tokens, text_tokens=text_tokens, image_modulation=image_modulation, text_modulation=text_modulation, image_projection=image_projection, text_projection=text_projection, image_merge=image_merge, text_merge=text_merge, norm_gains=norm_gains)


norm_epsilon = 1e-06

def layer_norm(tokens, modulation):
    tokens = tokens.astype(jnp.float32)
    centred = tokens - lax.optimization_barrier(jnp.mean(tokens, axis=1, keepdims=True))
    scaled = centred * lax.rsqrt(lax.optimization_barrier(jnp.mean(centred * centred, axis=1, keepdims=True)) + norm_epsilon)
    return (scaled * (1.0 + modulation[1]) + modulation[0]).astype(jnp.bfloat16)

def head_norm(features, gain):
    normed = features * lax.rsqrt(lax.optimization_barrier(jnp.mean(features * features, axis=-1, keepdims=True)) + norm_epsilon)
    return (normed * gain).astype(jnp.bfloat16)

def head_parts(projected, gain_query, gain_key):
    split = projected.reshape(projected.shape[0], HEADS, 3, HEAD_DIM)
    query = head_norm(split[:, :, 0], gain_query)
    keys = head_norm(split[:, :, 1], gain_key)
    values = split[:, :, 2].astype(jnp.bfloat16)
    return (query, keys, values)

def one_head(operands):
    query, keys, values = operands
    scores = jnp.dot(query, keys.T, preferred_element_type=jnp.float32) * HEAD_DIM ** (-0.5)
    peak = lax.optimization_barrier(jnp.max(scores, axis=1, keepdims=True))
    weights = jnp.exp(scores - peak)
    total = lax.optimization_barrier(jnp.sum(weights, axis=1, keepdims=True))
    mixed = jnp.dot(weights.astype(jnp.bfloat16), values, preferred_element_type=jnp.float32) / total
    return mixed.astype(jnp.bfloat16)

def reference(image_tokens, text_tokens, image_modulation, text_modulation, image_projection, text_projection, image_merge, text_merge, norm_gains):
    image_in = layer_norm(image_tokens, image_modulation)
    text_in = layer_norm(text_tokens, text_modulation)
    image_proj = jnp.dot(image_in, image_projection, preferred_element_type=jnp.float32)
    text_proj = jnp.dot(text_in, text_projection, preferred_element_type=jnp.float32)
    query_image, keys_image, values_image = head_parts(image_proj, norm_gains[0], norm_gains[1])
    query_text, keys_text, values_text = head_parts(text_proj, norm_gains[2], norm_gains[3])
    query_all = jnp.concatenate([query_image, query_text], axis=0).transpose(1, 0, 2)
    keys_all = jnp.concatenate([keys_image, keys_text], axis=0).transpose(1, 0, 2)
    values_all = jnp.concatenate([values_image, values_text], axis=0).transpose(1, 0, 2)
    attended = lax.map(one_head, (query_all, keys_all, values_all))
    attended = attended.transpose(1, 0, 2).reshape(IMAGE + TEXT, HEADS * HEAD_DIM)
    attn_image = attended[:IMAGE]
    attn_text = attended[IMAGE:]
    group_width = HEADS // N_TP * HEAD_DIM

    def add_group(summed, index):
        block = lax.dynamic_slice_in_dim(attn_image, index * group_width, group_width, 1)
        merge_rows = lax.dynamic_slice_in_dim(image_merge, index * group_width, group_width, 0)
        partial_value = jnp.dot(block, merge_rows, preferred_element_type=jnp.float32).astype(jnp.bfloat16)
        partial_value = lax.optimization_barrier(partial_value)
        return (summed + partial_value.astype(jnp.float32), None)
    summed, unused = lax.scan(add_group, jnp.zeros((IMAGE, D), jnp.float32), jnp.arange(N_TP, dtype=jnp.int32))
    image_update = (image_modulation[2] * summed).astype(jnp.bfloat16)
    text_sum = jnp.dot(attn_text, text_merge, preferred_element_type=jnp.float32)
    text_update = (text_modulation[2] * text_sum).astype(jnp.bfloat16)
    return (image_update, text_update)
```

```python
import jax
import jax.numpy as jnp
from jax import lax
from jax.experimental import pallas as pl
from jax.experimental.pallas import tpu as pltpu
from jax.sharding import PartitionSpec as P

HEAD_DIM = 128
D = 3072
EPS = 1e-06
NX, NZ, NY, NCTX, NTP = 4, 4, 8, 16, 16
ROWS = 32
TROWS = 16
CHUNKS = ((0,), (1, 7), (2, 6), (3, 5), (4,))
START = (0, 64, 192, 320, 448)
COUNT = (64, 128, 128, 128, 64)
NQ = 512 + TROWS
F32, BF16 = jnp.float32, jnp.bfloat16
LOG2E = 1.4426950408889634


def offset(r, h):
    for c, members in enumerate(CHUNKS):
        if r in members:
            return START[c] + (h * len(members) + members.index(r)) * ROWS


def layer_norm(tokens, modulation):
    tokens = tokens.astype(F32)
    centred = tokens - jnp.mean(tokens, axis=1, keepdims=True)
    scaled = centred * lax.rsqrt(jnp.mean(centred * centred, axis=1, keepdims=True) + EPS)
    return (scaled * (1.0 + modulation[1:2]) + modulation[0:1]).astype(BF16)


def head_norm(features, gain):
    normed = features * lax.rsqrt(jnp.mean(features * features, axis=1, keepdims=True) + EPS)
    return (normed * gain).astype(BF16)


def arrived(ref, sem):
    pltpu.make_async_copy(ref, ref, sem).wait()


def kernel(
    img, txt, imod, tmod, wp_in, wt, wm_in, wtm, gains,
    out_i, out_t,
    g, wp, w2, kv, kvt, q, tf, tsl, tpart, trcv, o, ox, to, top, tor, rr, rl, sr, sl,
    local_sem, a_send, a_recv, z_send, z_recv, x_send, x_recv,
    ts_send, ts_recv, tp_send, tp_recv, tk_send, tk_recv, to_send, to_recv, tm_send, tm_recv,
    w_send, w_recv, o_send, o_recv, r_send, r_recv,
):
    ctx, tp, dp = lax.axis_index("ctx"), lax.axis_index("tp"), lax.axis_index("dp")
    x, z = lax.rem(ctx, NX), lax.div(ctx, NX)
    y, hi = lax.rem(tp, NY), lax.div(tp, NY)
    mirror = {"ctx": (NZ - 1 - z) * NX + x, "tp": lax.rem(tp + NY, NTP)}
    y_left = {"tp": hi * NY + lax.rem(y + NY - 1, NY)}
    y_right = {"tp": hi * NY + lax.rem(y + 1, NY)}
    x_left = {"ctx": z * NX + lax.rem(x + NX - 1, NX)}
    x_right = {"ctx": z * NX + lax.rem(x + 1, NX)}
    other_core = {"dp": 1 - dp}
    pending = []

    def send(src, dst, ss, rs, device, when=None):
        def go():
            pltpu.make_async_remote_copy(
                src_ref=src, dst_ref=dst, send_sem=ss, recv_sem=rs,
                device_id=device, device_id_type=pl.DeviceIdType.MESH,
            ).start()

        if when is None:
            go()
        else:
            pl.when(when)(go)
        pending.append((src, ss, when))

    def peers(axis, own, count, act):
        def step(i, carry):
            act(lax.rem(own + i, count))
            return carry

        lax.fori_loop(1, count, step, 0)

    barrier = pltpu.get_barrier_semaphore()

    def greet(device):
        pl.semaphore_signal(barrier, inc=1, device_id=device, device_id_type=pl.DeviceIdType.MESH)

    peers("tp", tp, NTP, lambda i: greet({"tp": i}))
    peers("ctx", ctx, NCTX, lambda i: greet({"ctx": i}))
    greet(mirror)
    greet(other_core)

    load_wp = pltpu.make_async_copy(wp_in, wp, local_sem.at[0])
    load_wp.start()
    load_wm = pltpu.make_async_copy(wm_in, w2.at[pl.ds(0, HEAD_DIM)], local_sem.at[1])
    load_wm.start()

    g[0:ROWS, :] = layer_norm(img[...], imod[...])
    tf[...] = layer_norm(txt[...], tmod[...]).astype(F32)

    def columns_of(ref, rows, who):
        base = pl.multiple_of(lax.div(who * 3, 2) * 128, 128)
        wide = ref[rows, pl.ds(base, 256)]
        return jnp.where(lax.rem(who, 2) == 1, pltpu.roll(wide, 192, 1), wide)

    tsl[tp] = columns_of(tf, slice(0, TROWS), ctx).astype(BF16)

    pl.semaphore_wait(barrier, 2 * (NTP - 1) + 2)

    def rows_of(r, h, part=None):
        if part is None:
            return g.at[pl.ds(offset(r, h), ROWS)]
        return g.at[pl.ds(offset(r, h) + part * (ROWS // 2), ROWS // 2)]

    def forward(r, h, side):
        device = y_left if side == 0 else y_right
        there = r + 1 if side == 0 else (r + NY - 1) % NY
        hop = r if side == 0 else (NY - r) % NY
        if there == 4:
            send(rows_of(r, h, side), rows_of(4, h, side), a_send.at[side, hop, h], a_recv.at[4 + 4 * side, h], device)
        else:
            send(rows_of(r, h), rows_of(there, h), a_send.at[side, hop, h], a_recv.at[there, h], device)

    send(rows_of(0, 0), rows_of(0, 1), a_send.at[0, 4, 0], a_recv.at[0, 1], mirror)
    forward(0, 0, 0)
    forward(0, 0, 1)

    def send_text(i):
        pltpu.make_async_remote_copy(
            src_ref=tsl.at[tp], dst_ref=tsl.at[tp], send_sem=ts_send.at[i], recv_sem=ts_recv.at[tp],
            device_id={"tp": i}, device_id_type=pl.DeviceIdType.MESH,
        ).start()

    peers("tp", tp, NTP, send_text)

    piece = x * 2 + dp

    def merge_piece(p):
        return w2.at[pl.ds(pl.multiple_of(HEAD_DIM + p * 16, 16), 16)]

    load_wm.wait()
    send(w2.at[pl.ds(pl.multiple_of(piece * 16, 16), 16)], merge_piece(piece), w_send.at[0], w_recv.at[0], mirror)

    arrived(rows_of(0, 1), a_recv.at[0, 1])
    forward(0, 1, 0)
    forward(0, 1, 1)

    gain = [gains[i : i + 1, :] for i in range(4)]

    def project(c):
        rows = pl.ds(START[c], COUNT[c])
        out = jnp.dot(g[rows, :], wp[...], preferred_element_type=F32)
        q[rows, :] = head_norm(out[:, 0:128], gain[0])
        kv[z * NX, rows, 0:128] = head_norm(out[:, 128:256], gain[1])
        kv[z * NX, rows, 128:256] = out[:, 256:384].astype(BF16)

    def kv_rows(zs, rx, c, part=None):
        count = COUNT[c] if part is None else COUNT[c] // 2
        return kv.at[zs * NX + rx, pl.ds(START[c] + (0 if part is None else part * count), count)]

    def z_hop(c, zs, up):
        to_z = z + 1 if up else z - 1
        valid = (z < NZ - 1) if up else (z > 0)
        return to_z, valid

    def send_z(c, k, up):
        zs = z - k if up else z + k
        to_z = z + 1 if up else z - 1
        ok = (zs >= 0) & (to_z < NZ) if up else (zs < NZ) & (to_z >= 0)
        where = kv_rows(zs, 0, c)
        send(where, where, z_send.at[c, k, int(up)], z_recv.at[c, zs], {"ctx": to_z * NX + x}, ok)

    def source(k):
        return (z - k, z - k >= 0), (z + k, z + k < NZ)

    def send_x(c, zs, ok):
        mine = kv_rows(zs, 0, c)
        send(mine, kv_rows(zs, 1, c), x_send.at[c, zs, 0], x_recv.at[c, zs, 0], x_left, ok)
        send(mine, kv_rows(zs, 3, c), x_send.at[c, zs, 1], x_recv.at[c, zs, 1], x_right, ok)

    def pass_x(c, zs, ok):
        def wait(rx, i):
            arrived(kv_rows(zs, rx, c), x_recv.at[c, zs, i])

        if ok is None:
            wait(1, 0)
        else:
            pl.when(ok)(lambda: wait(1, 0))
        send(kv_rows(zs, 1, c, 0), kv_rows(zs, 2, c, 0), x_send.at[c, zs, 2], x_recv.at[c, zs, 2], x_left, ok)
        if ok is None:
            wait(3, 1)
        else:
            pl.when(ok)(lambda: wait(3, 1))
        send(kv_rows(zs, 3, c, 1), kv_rows(zs, 2, c, 1), x_send.at[c, zs, 3], x_recv.at[c, zs, 3], x_right, ok)

    def stage(c, n):
        if n == 0:
            send_z(c, 0, True)
            send_z(c, 0, False)
            send_x(c, z, None)
        elif n <= 3:
            for up, (zs, ok) in zip((True, False), source(n)):
                pl.when(ok)(lambda: arrived(kv_rows(zs, 0, c), z_recv.at[c, zs]))
                if n < 3:
                    send_z(c, n, up)
                send_x(c, zs, ok)
        elif n == 4:
            pass_x(c, z, None)
        else:
            for zs, ok in source(n - 4):
                pass_x(c, zs, ok)

    arrived(wp, local_sem.at[0])
    project(0)
    stage(0, 0)

    peers("tp", tp, NTP, lambda i: arrived(tsl.at[i], ts_recv.at[i]))
    text_part = jnp.dot(
        tsl[...].reshape(NTP * TROWS, 256)[:, 0:192], wt[...], preferred_element_type=F32
    )
    tpart[...] = text_part.reshape(NCTX, TROWS, 384)

    def send_part(i):
        pltpu.make_async_remote_copy(
            src_ref=tpart.at[i], dst_ref=trcv.at[ctx], send_sem=tp_send.at[i], recv_sem=tp_recv.at[ctx],
            device_id={"ctx": i}, device_id_type=pl.DeviceIdType.MESH,
        ).start()

    peers("ctx", ctx, NCTX, send_part)

    def merge_weights(step):
        if step == 0:
            arrived(merge_piece(piece), w_recv.at[0])
            for i in range(1, NX):
                send(
                    merge_piece(piece), merge_piece(piece), w_send.at[i], w_recv.at[i],
                    {"ctx": z * NX + lax.rem(x + i, NX)},
                )
        elif step == 1:
            for i in range(1, NX):
                theirs = lax.rem(x + NX - i, NX) * 2 + dp
                arrived(merge_piece(theirs), w_recv.at[i])
            for i in range(NX):
                p = i * 2 + dp
                send(merge_piece(p), merge_piece(p), w_send.at[4 + i], w_recv.at[4 + i], other_core)
        else:
            for i in range(NX):
                arrived(merge_piece(i * 2 + 1 - dp), w_recv.at[4 + i])

    def text_heads():
        peers("ctx", ctx, NCTX, lambda i: arrived(trcv.at[i], tp_recv.at[i]))
        trcv[ctx] = tpart[ctx]
        total = jnp.sum(trcv[...], axis=0)
        q[512:NQ, :] = head_norm(total[:, 0:128], gain[2])
        mine = pl.ds(pl.multiple_of(ctx * TROWS, TROWS), TROWS)
        kvt[mine, 0:128] = head_norm(total[:, 128:256], gain[3])
        kvt[mine, 128:256] = total[:, 256:384].astype(BF16)

        def send_keys(i):
            pltpu.make_async_remote_copy(
                src_ref=kvt.at[mine], dst_ref=kvt.at[mine], send_sem=tk_send.at[i], recv_sem=tk_recv.at[ctx],
                device_id={"ctx": i}, device_id_type=pl.DeviceIdType.MESH,
            ).start()

        peers("ctx", ctx, NCTX, send_keys)

    for d in (1, 2, 3):
        for h in (0, 1):
            arrived(rows_of(d, h), a_recv.at[d, h])
            forward(d, h, 0)
            arrived(rows_of(NY - d, h), a_recv.at[NY - d, h])
            forward(NY - d, h, 1)
            if h == 0:
                stage(d - 1, 1)
        project(d)
        stage(d, 0)
        for n in (2, 3, 4, 5, 6, 7):
            stage(d - 1, n)
        if d == 1:
            merge_weights(0)
            text_heads()
        if d == 2:
            merge_weights(1)
    for h in (0, 1):
        arrived(rows_of(4, h, 0), a_recv.at[4, h])
        arrived(rows_of(4, h, 1), a_recv.at[8, h])
    project(4)
    stage(4, 0)
    for n in (1, 2, 3, 4, 5, 6, 7):
        stage(3, n)
    for n in (1, 2, 3, 4, 5, 6, 7):
        stage(4, n)

    def last_x(c, zs, ok):
        def wait():
            arrived(kv_rows(zs, 2, c, 0), x_recv.at[c, zs, 2])
            arrived(kv_rows(zs, 2, c, 1), x_recv.at[c, zs, 3])

        if ok is None:
            wait()
        else:
            pl.when(ok)(wait)

    for c in range(5):
        last_x(c, z, None)
        for k in (1, 2, 3):
            for zs, ok in source(k):
                last_x(c, zs, ok)

    def text_rows(i):
        return kvt.at[pl.ds(pl.multiple_of(i * TROWS, TROWS), TROWS)]

    peers("ctx", ctx, NCTX, lambda i: arrived(text_rows(i), tk_recv.at[i]))
    merge_weights(2)

    scale = HEAD_DIM**-0.5 * LOG2E

    def attend(first, count):
        query = q[pl.ds(first, count), :]

        def block(carry, keys, values):
            best, total, weighted = carry
            s = lax.dot_general(query, keys, (((1,), (1,)), ((), ())), preferred_element_type=F32)
            fresh = jnp.maximum(best, jnp.max(s, axis=1, keepdims=True))
            decay = jnp.exp2((best - fresh) * scale)
            weights = jnp.exp2((s - fresh) * scale)
            total = total * decay + jnp.sum(weights, axis=1, keepdims=True)
            weighted = weighted * decay + jnp.dot(weights.astype(BF16), values, preferred_element_type=F32)
            return fresh, total, weighted

        carry = (
            jnp.full((count, 1), -1e30, F32),
            jnp.zeros((count, 1), F32),
            jnp.zeros((count, HEAD_DIM), F32),
        )
        carry = block(carry, kvt[:, 0:128], kvt[:, 128:256])

        def step(i, carry):
            both = kv[pl.ds(i * 2, 2)].reshape(1024, 256)
            return block(carry, both[:, 0:128], both[:, 128:256])

        best, total, weighted = lax.fori_loop(0, 8, step, carry)
        return (weighted / total).astype(BF16)

    def merge(c):
        rows = COUNT[c] // 2
        return jnp.dot(o[pl.ds(START[c] // 2, rows), :], w2[...], preferred_element_type=F32)

    def exchange(c):
        half = COUNT[c] // 2
        rows = pl.ds(START[c] // 2, half)
        count = COUNT[c] + (TROWS if c == 4 else 0)
        mixed = attend(START[c], count)
        o[rows, 0:128] = mixed[0:half]
        ox[rows, :] = mixed[half : 2 * half]
        send(ox.at[rows], o.at[rows, pl.ds(128, 128)], o_send.at[c], o_recv.at[c], mirror)
        if c == 4:
            to[ctx] = mixed[2 * half :]

            def send_out(i):
                pltpu.make_async_remote_copy(
                    src_ref=to.at[ctx], dst_ref=to.at[ctx], send_sem=to_send.at[i], recv_sem=to_recv.at[ctx],
                    device_id={"ctx": i}, device_id_type=pl.DeviceIdType.MESH,
                ).start()

            peers("ctx", ctx, NCTX, send_out)

    def text_merge():
        peers("ctx", ctx, NCTX, lambda i: arrived(to.at[i], to_recv.at[i]))
        part = jnp.dot(to[...].reshape(NCTX * TROWS, HEAD_DIM), wtm[...], preferred_element_type=F32)
        top[:, :, 0:192] = part.reshape(NTP, TROWS, 192)
        top[:, :, 192:256] = jnp.zeros((NTP, TROWS, 64), F32)

        def send_sum(i):
            pltpu.make_async_remote_copy(
                src_ref=top.at[i], dst_ref=tor.at[tp], send_sem=tm_send.at[i], recv_sem=tm_recv.at[tp],
                device_id={"tp": i}, device_id_type=pl.DeviceIdType.MESH,
            ).start()

        peers("tp", tp, NTP, send_sum)

    def reduce(c):
        rows = pl.ds(START[c] // 2, COUNT[c] // 2)
        arrived(o.at[rows, pl.ds(128, 128)], o_recv.at[c])
        part = merge(c)
        half = ROWS // 2
        if c == 4:
            sr[3, 0:half, :] = part[0:half].astype(BF16)
            sl[3, 0:half, :] = part[half:].astype(BF16)
            send(sr.at[3, pl.ds(0, half)], rr.at[3, pl.ds(0, half)], r_send.at[0, 3], r_recv.at[0, 3], y_right)
            send(sl.at[3, pl.ds(0, half)], rl.at[3, pl.ds(0, half)], r_send.at[1, 3], r_recv.at[1, 3], y_left)
            return
        if c == 0:
            arrived(rr.at[0], r_recv.at[0, 0])
            arrived(rl.at[0], r_recv.at[1, 0])
            total = part + rr[0].astype(F32) + rl[0].astype(F32)
            out_i[...] = (imod[2:3, :] * total).astype(BF16)
            return
        if c == 3:
            arrived(rr.at[3, pl.ds(0, half)], r_recv.at[0, 3])
            sr[2, 0:half, :] = (part[0:half] + rr[3, 0:half, :].astype(F32)).astype(BF16)
            sr[2, half:, :] = part[half:ROWS].astype(BF16)
        else:
            arrived(rr.at[c], r_recv.at[0, c])
            sr[c - 1] = (part[0:ROWS] + rr[c].astype(F32)).astype(BF16)
        send(sr.at[c - 1], rr.at[c - 1], r_send.at[0, c - 1], r_recv.at[0, c - 1], y_right)
        if c == 3:
            arrived(rl.at[3, pl.ds(0, half)], r_recv.at[1, 3])
            sl[2, 0:half, :] = part[ROWS : ROWS + half].astype(BF16)
            sl[2, half:, :] = (part[ROWS + half :] + rl[3, 0:half, :].astype(F32)).astype(BF16)
        else:
            arrived(rl.at[c], r_recv.at[1, c])
            sl[c - 1] = (part[ROWS:] + rl[c].astype(F32)).astype(BF16)
        send(sl.at[c - 1], rl.at[c - 1], r_send.at[1, c - 1], r_recv.at[1, c - 1], y_left)

    exchange(4)
    exchange(3)
    reduce(4)
    text_merge()
    exchange(2)
    reduce(3)
    exchange(1)
    reduce(2)
    exchange(0)
    reduce(1)

    peers("tp", tp, NTP, lambda i: arrived(tor.at[i], tm_recv.at[i]))
    tor[tp] = top[tp]
    text_total = jnp.sum(tor[...], axis=0)[:, 0:192]
    tf[0:3, :] = tmod[...]
    gate = columns_of(tf, slice(2, 3), ctx)[:, 0:192]
    out_t[...] = (gate * text_total).astype(BF16)

    reduce(0)

    for src, sem, when in pending:
        if when is None:
            arrived(src, sem)
        else:
            pl.when(when)(lambda: arrived(src, sem))
    peers("tp", tp, NTP, lambda i: arrived(tsl.at[tp], ts_send.at[i]))
    peers("ctx", ctx, NCTX, lambda i: arrived(tpart.at[i], tp_send.at[i]))
    peers("ctx", ctx, NCTX, lambda i: arrived(text_rows(ctx), tk_send.at[i]))
    peers("ctx", ctx, NCTX, lambda i: arrived(to.at[ctx], to_send.at[i]))
    peers("tp", tp, NTP, lambda i: arrived(top.at[i], tm_send.at[i]))


def on_device(*arrays):
    dma = pltpu.SemaphoreType.DMA
    vmem = pl.BlockSpec(memory_space=pltpu.VMEM)
    hbm = pl.BlockSpec(memory_space=pl.ANY)
    return pl.pallas_call(
        kernel,
        out_shape=(
            jax.ShapeDtypeStruct((ROWS, D), BF16),
            jax.ShapeDtypeStruct((TROWS, 192), BF16),
        ),
        in_specs=[vmem, vmem, vmem, vmem, hbm, vmem, hbm, vmem, vmem],
        out_specs=(vmem, vmem),
        scratch_shapes=[
            pltpu.VMEM((512, D), BF16),
            pltpu.VMEM((D, 384), BF16),
            pltpu.VMEM((256, D), BF16),
            pltpu.VMEM((NCTX, 512, 256), BF16),
            pltpu.VMEM((NCTX * TROWS, 256), BF16),
            pltpu.VMEM((NQ, HEAD_DIM), BF16),
            pltpu.VMEM((TROWS, D), F32),
            pltpu.VMEM((NTP, TROWS, 256), BF16),
            pltpu.VMEM((NCTX, TROWS, 384), F32),
            pltpu.VMEM((NCTX, TROWS, 384), F32),
            pltpu.VMEM((256, 256), BF16),
            pltpu.VMEM((256, HEAD_DIM), BF16),
            pltpu.VMEM((NCTX, TROWS, HEAD_DIM), BF16),
            pltpu.VMEM((NTP, TROWS, 256), F32),
            pltpu.VMEM((NTP, TROWS, 256), F32),
            pltpu.VMEM((4, ROWS, D), BF16),
            pltpu.VMEM((4, ROWS, D), BF16),
            pltpu.VMEM((4, ROWS, D), BF16),
            pltpu.VMEM((4, ROWS, D), BF16),
            dma((2,)),
            dma((2, 5, 2)),
            dma((9, 2)),
            dma((5, 3, 2)),
            dma((5, NZ)),
            dma((5, NZ, 4)),
            dma((5, NZ, 4)),
            dma((NTP,)), dma((NTP,)),
            dma((NCTX,)), dma((NCTX,)),
            dma((NCTX,)), dma((NCTX,)),
            dma((NCTX,)), dma((NCTX,)),
            dma((NTP,)), dma((NTP,)),
            dma((8,)), dma((8,)),
            dma((5,)), dma((5,)),
            dma((2, 4)), dma((2, 4)),
        ],
        compiler_params=pltpu.CompilerParams(
            collective_id=0, has_side_effects=True, vmem_limit_bytes=48 * 1024 * 1024
        ),
        cost_estimate=pl.CostEstimate(flops=7_000_000_000, bytes_accessed=8_000_000, transcendentals=4_500_000),
        name="joint_attention",
    )(*arrays)


def solution(mesh):
    placed = (
        P(("dp", "ctx", "tp"), None),
        P(("dp", "tp"), None),
        P("dp", None),
        P("dp", None),
        P(None, "tp"),
        P("ctx", "tp"),
        P("tp", None),
        P("tp", "ctx"),
        P(),
    )
    return jax.shard_map(
        on_device,
        mesh=mesh,
        in_specs=placed,
        out_specs=(P(("dp", "ctx", "tp"), None), P(("dp", "tp"), "ctx")),
        check_vma=False,
    )
```

```python
import jax
import jax.numpy as jnp
from jax import lax
from jax.experimental import pallas as pl
from jax.experimental.pallas import tpu as pltpu
from jax.sharding import PartitionSpec as P

HEAD_DIM = 128
D = 3072
EPS = 1e-06
DW = D + 128
NX, NZ, NY, NCTX, NTP = 4, 4, 8, 16, 16
ROWS = 32
TROWS = 16
CHUNKS = (
    ((0, 0), (1, 0), (7, 0)),
    ((2, 0), (6, 0), (0, 1)),
    ((3, 0), (5, 0), (4, 0)),
    ((1, 1), (7, 1)),
    ((2, 1), (6, 1)),
    ((3, 1), (5, 1)),
    ((4, 1),),
)
COUNT = tuple(32 * len(members) for members in CHUNKS)
START = tuple(sum(COUNT[:c]) for c in range(len(CHUNKS)))
NCH = len(CHUNKS)
RING = ((0,), (1, 7), (2, 6), (3, 5), (4,))
RSTART = (0, 32, 96, 160, 224)
RCOUNT = (32, 64, 64, 64, 32)
NQ = 512 + TROWS
F32, BF16 = jnp.float32, jnp.bfloat16
LOG2E = 1.4426950408889634


def offset(r, h):
    for c, members in enumerate(CHUNKS):
        if (r, h) in members:
            return START[c] + members.index((r, h)) * ROWS


def layer_norm(tokens, modulation):
    tokens = tokens.astype(F32)
    centred = tokens - jnp.mean(tokens, axis=1, keepdims=True)
    scaled = centred * lax.rsqrt(jnp.mean(centred * centred, axis=1, keepdims=True) + EPS)
    return (scaled * (1.0 + modulation[1:2]) + modulation[0:1]).astype(BF16)


def head_norm(features, gain):
    normed = features * lax.rsqrt(jnp.mean(features * features, axis=1, keepdims=True) + EPS)
    return (normed * gain).astype(BF16)


def arrived(ref, sem):
    pltpu.make_async_copy(ref, ref, sem).wait()


def kernel(
    img_in, txt_in, imod_in, tmod_in, wp_in, wt_in, wm_in, wtm_in, gains_in,
    out_i, out_t,
    img, txt, imod, tmod, wt, wtm, gains,
    g, gm, wp, w2, kv, kvt, q, tf, tpart, trcv, best_s, total_s, acc_s, o, ox, to, top, tfar, tor, rr, rl, sr, sl,
    local_sem, a_send, a_recv, z_send, z_recv, x_send, x_recv,
    tp_send, tp_recv, tk_send, tk_recv, to_send, to_recv, tm_send, tm_recv, far_send, far_recv,
    w_send, w_recv, o_send, o_recv, r_send, r_recv,
):
    ctx, tp, dp = lax.axis_index("ctx"), lax.axis_index("tp"), lax.axis_index("dp")
    x, z = lax.rem(ctx, NX), lax.div(ctx, NX)
    y, hi = lax.rem(tp, NY), lax.div(tp, NY)
    mirror_ctx = (NZ - 1 - z) * NX + x
    mirror = {"ctx": mirror_ctx, "tp": lax.rem(tp + NY, NTP)}
    far = {"tp": lax.rem(tp + NY, NTP)}
    y_left = {"tp": hi * NY + lax.rem(y + NY - 1, NY)}
    y_right = {"tp": hi * NY + lax.rem(y + 1, NY)}
    x_left = {"ctx": z * NX + lax.rem(x + NX - 1, NX)}
    x_right = {"ctx": z * NX + lax.rem(x + 1, NX)}
    other_core = {"dp": 1 - dp}
    def start(src, dst, ss, rs, device):
        pltpu.make_async_remote_copy(
            src_ref=src, dst_ref=dst, send_sem=ss, recv_sem=rs,
            device_id=device, device_id_type=pl.DeviceIdType.MESH,
        ).start()

    def ctx_peers(act):
        def step(i, carry):
            act(lax.rem(ctx + i, NCTX))
            return carry

        lax.fori_loop(1, NCTX, step, 0)

    barrier = pltpu.get_barrier_semaphore()

    def greet(device):
        pl.semaphore_signal(barrier, inc=1, device_id=device, device_id_type=pl.DeviceIdType.MESH)

    greet(mirror)
    greet(far)
    ctx_peers(lambda i: greet({"ctx": i}))
    for i in range(1, NY):
        greet({"tp": hi * NY + lax.rem(y + i, NY)})
    greet(other_core)

    loads = []
    wanted = (
        (img_in, img), (txt_in, txt), (imod_in, imod), (tmod_in, tmod), (gains_in, gains),
        (wp_in, wp), (wt_in, wt.at[pl.ds(0, 192)]), (wm_in, w2.at[pl.ds(0, HEAD_DIM)]), (wtm_in, wtm),
    )
    for i, (src, dst) in enumerate(wanted):
        loads.append(pltpu.make_async_copy(src, dst, local_sem.at[i]))
        loads[-1].start()
    for i in range(4):
        loads[i].wait()
    wt[192:256, :] = jnp.zeros((64, 384), BF16)

    normed = layer_norm(img[...], imod[...])
    g[0:ROWS, 0:D] = normed
    gm[:, 0:D] = normed
    tf[...] = layer_norm(txt[...], tmod[...]).astype(F32)

    def columns_of(ref, rows, who):
        base = pl.multiple_of(lax.div(who * 3, 2) * 128, 128)
        wide = ref[rows, pl.ds(base, 256)]
        return jnp.where(lax.rem(who, 2) == 1, pltpu.roll(wide, 192, 1), wide)

    for ref, who in ((g, ctx), (gm, mirror_ctx)):
        columns = columns_of(tf, slice(0, TROWS), who).astype(BF16)
        ref[0:16, D:DW] = columns[:, 0:128]
        ref[16:32, D:DW] = columns[:, 128:256]

    pl.semaphore_wait(barrier, (NCTX - 1) + (NY - 1) + 3)

    def rows_of(r, h, p):
        return g.at[pl.ds(offset(r, h) + p * 16, 16)]

    def forward(r, h, side, p):
        there = r + 1 if side == 0 else (r + NY - 1) % NY
        if there == 4 and p != side:
            return
        start(
            rows_of(r, h, p), rows_of(there, h, p), a_send, a_recv.at[there, h, p],
            y_left if side == 0 else y_right,
        )

    for p in (0, 1):
        start(gm.at[pl.ds(p * 16, 16)], rows_of(0, 1, p), a_send, a_recv.at[0, 1, p], mirror)
        forward(0, 0, 0, p)
        forward(0, 0, 1, p)

    def tokens(r, h, p):
        if r == 0:
            arrived(rows_of(0, h, p), a_recv.at[0, h, p])
            forward(0, h, 0, p)
            forward(0, h, 1, p)
        elif r == 4:
            arrived(rows_of(4, h, p), a_recv.at[4, h, p])
        else:
            arrived(rows_of(r, h, p), a_recv.at[r, h, p])
            forward(r, h, 0, p)
            arrived(rows_of(NY - r, h, p), a_recv.at[NY - r, h, p])
            forward(NY - r, h, 1, p)

    def gain(i):
        return gains[i : i + 1, :]

    def project(c):
        rows = pl.ds(START[c], COUNT[c])
        out = jnp.dot(g[rows, 0:D], wp[...], preferred_element_type=F32)
        q[rows, :] = head_norm(out[:, 0:128], gain(0))
        kv[0, rows, 0:128] = head_norm(out[:, 128:256], gain(1))
        kv[0, rows, 128:256] = out[:, 256:384].astype(BF16)

    def text_project(c):
        blocks = COUNT[c] // ROWS
        columns = g[pl.ds(START[c], COUNT[c]), D:DW].reshape(blocks, 2, 16, 128)
        columns = jnp.concatenate([columns[:, 0], columns[:, 1]], axis=2).reshape(blocks * 16, 256)
        out = jnp.dot(columns, wt[...], preferred_element_type=F32)
        for b, (r, h) in enumerate(CHUNKS[c]):
            slot = r * 2 + h
            tpart[slot] = out[b * 16 : b * 16 + 16].astype(BF16)
            target = lax.rem(h + hi, 2) * NY + lax.rem(y + r, NY)

            @pl.when(target != ctx)
            def _():
                start(tpart.at[slot], trcv.at[ctx], tp_send, tp_recv, {"ctx": target})

    def kv_rows(k, r, c, part=None):
        count = COUNT[c] if part is None else COUNT[c] // 2
        return kv.at[k * NX + r, pl.ds(START[c] + (0 if part is None else part * count), count)]

    def send_x(c, k):
        start(kv_rows(k, 0, c), kv_rows(k, 1, c), x_send, x_recv.at[c, k, 0], x_left)
        start(kv_rows(k, 0, c), kv_rows(k, 3, c), x_send, x_recv.at[c, k, 1], x_right)

    def spread(c):
        for k in (1, 3, 2):
            device = {"ctx": lax.rem(z + k, NZ) * NX + x}
            start(kv_rows(0, 0, c), kv_rows(NZ - k, 0, c), z_send, z_recv.at[c, NZ - k], device)
        send_x(c, 0)

    def across(c, k):
        arrived(kv_rows(k, 0, c), z_recv.at[c, k])
        send_x(c, k)

    def around(c, k):
        arrived(kv_rows(k, 1, c), x_recv.at[c, k, 0])
        start(kv_rows(k, 1, c, 0), kv_rows(k, 2, c, 0), x_send, x_recv.at[c, k, 2], x_left)
        arrived(kv_rows(k, 3, c), x_recv.at[c, k, 1])
        start(kv_rows(k, 3, c, 1), kv_rows(k, 2, c, 1), x_send, x_recv.at[c, k, 2], x_right)

    def complete(c):
        for k in range(NZ):
            arrived(kv_rows(k, 2, c), x_recv.at[c, k, 2])

    piece = x * 2 + dp

    def merge_piece(p):
        return w2.at[pl.ds(pl.multiple_of(HEAD_DIM + p * 16, 16), 16)]

    def merge_weights(step):
        if step == 0:
            loads[7].wait()
            start(w2.at[pl.ds(pl.multiple_of(piece * 16, 16), 16)], merge_piece(piece), w_send, w_recv.at[0], mirror)
        elif step == 1:
            arrived(merge_piece(piece), w_recv.at[0])
            for i in range(1, NX):
                start(
                    merge_piece(piece), merge_piece(piece), w_send, w_recv.at[1],
                    {"ctx": z * NX + lax.rem(x + i, NX)},
                )
        elif step == 2:
            arrived(w2.at[pl.ds(0, 48)], w_recv.at[1])
            for i in range(NX):
                p = i * 2 + dp
                start(merge_piece(p), merge_piece(p), w_send, w_recv.at[2], other_core)
        else:
            arrived(w2.at[pl.ds(0, 64)], w_recv.at[2])

    def text_rows(i):
        return kvt.at[pl.ds(pl.multiple_of(i * TROWS, TROWS), TROWS)]

    def text_heads():
        arrived(trcv.at[pl.ds(0, NCTX - 1)], tp_recv)
        own = lax.rem(lax.rem(ctx, NY) + NY - y, NY) * 2 + lax.rem(lax.div(ctx, NY) + hi, 2)
        trcv[ctx] = tpart[own]
        total = jnp.sum(trcv[...].astype(F32), axis=0)
        q[512:NQ, :] = head_norm(total[:, 0:128], gain(2))
        mine = pl.ds(pl.multiple_of(ctx * TROWS, TROWS), TROWS)
        kvt[mine, 0:128] = head_norm(total[:, 128:256], gain(3))
        kvt[mine, 128:256] = total[:, 256:384].astype(BF16)
        ctx_peers(lambda i: start(text_rows(ctx), text_rows(ctx), tk_send, tk_recv, {"ctx": i}))

    scale = HEAD_DIM**-0.5 * LOG2E

    def fold(state, query, key_blocks):
        best, total, weighted = state
        for both in key_blocks:
            s = lax.dot_general(query, both[:, 0:128], (((1,), (1,)), ((), ())), preferred_element_type=F32)
            fresh = jnp.maximum(best, jnp.max(s, axis=1, keepdims=True))
            decay = jnp.exp2((best - fresh) * scale)
            weights = jnp.exp2((s - fresh) * scale)
            total = total * decay + jnp.sum(weights, axis=1, keepdims=True)
            weighted = weighted * decay + jnp.dot(weights.astype(BF16), both[:, 128:256], preferred_element_type=F32)
            best = fresh
        return best, total, weighted

    def attend(first, end, low, high):
        rows = pl.ds(first, end - first)
        count = START[high] + COUNT[high] - START[low]
        both = kv[:, pl.ds(START[low], count)].reshape(NCTX * count, 256)
        state = fold((best_s[rows, :], total_s[rows, :], acc_s[rows, :]), q[rows, :], [both])
        best_s[rows, :], total_s[rows, :], acc_s[rows, :] = state

    def finish(c):
        first = RING[c][0]
        ranges = [(offset(first, h), RCOUNT[c]) for h in (0, 1)]
        if c == 4:
            ranges.append((512, TROWS))

        def rows_from(ref):
            return jnp.concatenate([ref[pl.ds(at, n), :] for at, n in ranges], axis=0)

        last = kv[:, pl.ds(START[NCH - 1], COUNT[NCH - 1])].reshape(NCTX * COUNT[NCH - 1], 256)
        state = (rows_from(best_s), rows_from(total_s), rows_from(acc_s))
        best, total, weighted = fold(state, rows_from(q), [last, kvt[...]])
        return (weighted / total).astype(BF16)

    best_s[...] = jnp.full((NQ, 1), -1e30, F32)
    total_s[...] = jnp.zeros((NQ, 1), F32)
    acc_s[...] = jnp.zeros((NQ, HEAD_DIM), F32)

    def enter(c):
        project(c)
        spread(c)
        text_project(c)

    tokens(1, 0, 0)
    tokens(1, 0, 1)
    for i in (4, 5, 6):
        loads[i].wait()
    enter(0)
    tokens(0, 1, 0)
    tokens(2, 0, 0)
    tokens(2, 0, 1)
    around(0, 0)
    tokens(0, 1, 1)
    enter(1)
    tokens(1, 1, 0)
    across(0, 3)
    merge_weights(0)
    across(0, 1)
    tokens(3, 0, 0)
    across(0, 2)
    around(1, 0)
    tokens(3, 0, 1)
    around(0, 3)
    across(1, 3)
    around(0, 1)
    across(1, 1)
    tokens(1, 1, 1)
    enter(3)
    around(0, 2)
    across(1, 2)
    around(1, 3)
    tokens(2, 1, 0)
    merge_weights(1)
    around(1, 1)
    tokens(4, 0, 0)
    tokens(4, 0, 1)
    enter(2)
    around(1, 2)
    around(3, 0)
    across(3, 1)
    across(3, 3)
    complete(0)
    tokens(2, 1, 1)
    enter(4)
    across(3, 2)
    merge_weights(2)
    tokens(3, 1, 0)
    around(2, 0)
    complete(1)
    attend(0, 288, 0, 1)
    tokens(3, 1, 1)
    enter(5)
    around(3, 1)
    around(3, 3)
    around(3, 2)
    around(4, 0)
    across(2, 1)
    tokens(4, 1, 0)
    tokens(4, 1, 1)
    enter(6)
    across(2, 3)
    across(2, 2)
    across(4, 3)
    attend(288, 512, 0, 1)
    around(5, 0)
    across(4, 1)
    across(4, 2)
    complete(3)
    around(2, 1)
    across(5, 3)
    around(6, 0)
    across(5, 1)
    around(2, 3)
    across(5, 2)
    around(2, 2)
    across(6, 3)
    around(4, 3)
    across(6, 1)
    across(6, 2)
    around(4, 1)
    around(4, 2)
    text_heads()
    around(5, 3)
    around(5, 1)
    around(5, 2)
    complete(2)
    attend(0, 512, 2, 2)
    around(6, 1)
    around(6, 3)
    around(6, 2)
    attend(512, 528, 0, 2)
    complete(4)
    attend(0, 528, 3, 4)
    complete(5)
    complete(6)
    attend(0, 528, 5, 5)
    arrived(kvt.at[pl.ds(0, (NCTX - 1) * TROWS)], tk_recv)
    merge_weights(3)

    def exchange(c):
        half = RCOUNT[c]
        rows = pl.ds(RSTART[c], half)
        mixed = finish(c)
        ox[rows, :] = mixed[half : 2 * half]
        start(ox.at[rows], o.at[rows, pl.ds(128, 128)], o_send, o_recv.at[c], mirror)
        o[rows, 0:128] = mixed[0:half]
        if c == 4:
            to[ctx] = mixed[2 * half :]
            ctx_peers(lambda i: start(to.at[ctx], to.at[ctx], to_send, to_recv, {"ctx": i}))

    def text_merge(step):
        if step == 0:
            arrived(to.at[pl.ds(0, NCTX - 1)], to_recv)
            loads[8].wait()
            part = lax.dot_general(
                to[...].reshape(NCTX * TROWS, HEAD_DIM), wtm[...], (((1,), (1,)), ((), ())), preferred_element_type=F32
            )
            top[:, :, 0:192] = part.reshape(NTP, TROWS, 192).astype(BF16)
            top[:, :, 192:256] = jnp.zeros((NTP, TROWS, 64), BF16)
            start(top.at[pl.ds((1 - hi) * NY, NY)], tfar, far_send, far_recv, far)
        elif step == 1:
            arrived(tfar, far_recv)
            tfar[...] = (tfar[...].astype(F32) + top[pl.ds(hi * NY, NY)].astype(F32)).astype(BF16)
            for i in range(1, NY):
                there = lax.rem(y + i, NY)
                start(tfar.at[there], tor.at[i], tm_send, tm_recv, {"tp": hi * NY + there})
        else:
            arrived(tor.at[pl.ds(1, NY - 1)], tm_recv)
            tor[0] = tfar[y]
            text_total = jnp.sum(tor[...].astype(F32), axis=0)[:, 0:192]
            tf[0:3, :] = tmod[...]
            gate = columns_of(tf, slice(2, 3), ctx)[:, 0:192]
            out_t[...] = (gate * text_total).astype(BF16)

    def merge(c):
        rows = pl.ds(RSTART[c], RCOUNT[c])
        arrived(o.at[rows, pl.ds(128, 128)], o_recv.at[c])
        return jnp.dot(o[rows, :], w2[...], preferred_element_type=F32)

    def reduce(c):
        part = merge(c)
        if c == 0:
            total = part
            for p in (0, 1):
                half = slice(p * 16, p * 16 + 16)
                for way, recv in enumerate((rr, rl)):
                    arrived(recv.at[0, pl.ds(p * 16, 16)], r_recv.at[way, 0, p])
                sums = part[half] + rr[0, half, :].astype(F32) + rl[0, half, :].astype(F32)
                out_i[half, :] = (imod[2:3, :] * sums).astype(BF16)
            return
        for turn in (0, 1):
            for way, recv, out, device in ((0, rr, sr, y_right), (1, rl, sl, y_left)):
                p = 1 - way if turn == 0 else way
                half = slice(p * 16, p * 16 + 16)
                ref = pl.ds(p * 16, 16)
                if c == 4:
                    if p != way:
                        continue
                    sums = part[half]
                else:
                    sums = part[way * ROWS + p * 16 : way * ROWS + p * 16 + 16]
                    if c < 3 or p == way:
                        arrived(recv.at[c, ref], r_recv.at[way, c, p])
                        sums = sums + recv[c, half, :].astype(F32)
                out[c - 1, half, :] = sums.astype(BF16)
                start(out.at[c - 1, ref], recv.at[c - 1, ref], r_send, r_recv.at[way, c - 1, p], device)

    exchange(4)
    exchange(3)
    reduce(4)
    exchange(2)
    reduce(3)
    text_merge(0)
    exchange(1)
    reduce(2)
    exchange(0)
    text_merge(1)
    reduce(1)
    text_merge(2)
    reduce(0)

    arrived(g.at[pl.ds(0, 480)], a_send)
    arrived(kv.at[pl.ds(0, 3)], z_send)
    arrived(kv.at[pl.ds(0, 12)], x_send)
    arrived(tpart.at[pl.ds(0, NCTX - 1)], tp_send)
    arrived(kvt.at[pl.ds(0, (NCTX - 1) * TROWS)], tk_send)
    arrived(to.at[pl.ds(0, NCTX - 1)], to_send)
    arrived(tfar, far_send)
    arrived(tor.at[pl.ds(0, NY - 1)], tm_send)
    arrived(w2.at[pl.ds(0, 128)], w_send)
    arrived(ox, o_send)
    arrived(w2.at[pl.ds(0, 224)], r_send)


def on_device(*arrays):
    arrays = arrays[:7] + (arrays[7].T,) + arrays[8:]
    dma = pltpu.SemaphoreType.DMA
    vmem = pl.BlockSpec(memory_space=pltpu.VMEM)
    hbm = pl.BlockSpec(memory_space=pltpu.HBM)
    return pl.pallas_call(
        kernel,
        out_shape=(
            jax.ShapeDtypeStruct((ROWS, D), BF16),
            jax.ShapeDtypeStruct((TROWS, 192), BF16),
        ),
        in_specs=[hbm] * 9,
        out_specs=(vmem, vmem),
        scratch_shapes=[
            pltpu.VMEM((ROWS, D), BF16),
            pltpu.VMEM((TROWS, D), BF16),
            pltpu.VMEM((3, D), F32),
            pltpu.VMEM((3, D), F32),
            pltpu.VMEM((256, 384), BF16),
            pltpu.VMEM((192, HEAD_DIM), BF16),
            pltpu.VMEM((4, HEAD_DIM), F32),
            pltpu.VMEM((512, DW), BF16),
            pltpu.VMEM((ROWS, DW), BF16),
            pltpu.VMEM((D, 384), BF16),
            pltpu.VMEM((256, D), BF16),
            pltpu.VMEM((NCTX, 512, 256), BF16),
            pltpu.VMEM((NCTX * TROWS, 256), BF16),
            pltpu.VMEM((NQ, HEAD_DIM), BF16),
            pltpu.VMEM((TROWS, D), F32),
            pltpu.VMEM((NTP, TROWS, 384), BF16),
            pltpu.VMEM((NCTX, TROWS, 384), BF16),
            pltpu.VMEM((NQ, 1), F32),
            pltpu.VMEM((NQ, 1), F32),
            pltpu.VMEM((NQ, HEAD_DIM), F32),
            pltpu.VMEM((256, 256), BF16),
            pltpu.VMEM((256, HEAD_DIM), BF16),
            pltpu.VMEM((NCTX, TROWS, HEAD_DIM), BF16),
            pltpu.VMEM((NTP, TROWS, 256), BF16),
            pltpu.VMEM((NY, TROWS, 256), BF16),
            pltpu.VMEM((NY, TROWS, 256), BF16),
            pltpu.VMEM((4, ROWS, D), BF16),
            pltpu.VMEM((4, ROWS, D), BF16),
            pltpu.VMEM((4, ROWS, D), BF16),
            pltpu.VMEM((4, ROWS, D), BF16),
            dma((9,)),
            dma,
            dma((NY, 2, 2)),
            dma,
            dma((NCH, NZ)),
            dma,
            dma((NCH, NZ, 3)),
            dma, dma,
            dma, dma,
            dma, dma,
            dma, dma,
            dma, dma,
            dma, dma((3,)),
            dma, dma((5,)),
            dma, dma((2, 4, 2)),
        ],
        compiler_params=pltpu.CompilerParams(
            collective_id=0, has_side_effects=True, vmem_limit_bytes=63 * 1024 * 1024
        ),
        cost_estimate=pl.CostEstimate(flops=7_000_000_000, bytes_accessed=8_000_000, transcendentals=4_500_000),
        name="joint_attention",
    )(*arrays)


def solution(mesh):
    placed = (
        P(("dp", "ctx", "tp"), None),
        P(("dp", "tp"), None),
        P("dp", None),
        P("dp", None),
        P(None, "tp"),
        P("ctx", "tp"),
        P("tp", None),
        P("tp", "ctx"),
        P(),
    )
    return jax.shard_map(
        on_device,
        mesh=mesh,
        in_specs=placed,
        out_specs=(P(("dp", "ctx", "tp"), None), P(("dp", "tp"), "ctx")),
        check_vma=False,
    )
```

```python
import jax
import jax.numpy as jnp
from jax import lax
from jax.experimental import pallas as pl
from jax.experimental.pallas import tpu as pltpu
from jax.sharding import PartitionSpec as P

HEAD_DIM = 128
D = 3072
EPS = 1e-06
HALF = D // 2
DW = D + 128
NX, NZ, NY, NCTX, NTP = 4, 4, 8, 16, 16
ROWS = 32
TROWS = 16
CHUNKS = (
    ((0, 0), (1, 0), (7, 0)),
    ((2, 0), (6, 0)),
    ((0, 1), (3, 0), (5, 0)),
    ((1, 1), (7, 1)),
    ((4, 0), (2, 1), (6, 1)),
    ((3, 1), (5, 1)),
    ((4, 1),),
)
COUNT = tuple(32 * len(members) for members in CHUNKS)
START = tuple(sum(COUNT[:c]) for c in range(len(CHUNKS)))
NCH = len(CHUNKS)
RING = ((0,), (1, 7), (2, 6), (3, 5), (4,))
RSTART = (0, 32, 96, 160, 224)
RCOUNT = (32, 64, 64, 64, 32)
NQ = 512 + TROWS
F32, BF16 = jnp.float32, jnp.bfloat16
LOG2E = 1.4426950408889634


def offset(r, h):
    for c, members in enumerate(CHUNKS):
        if (r, h) in members:
            return START[c] + members.index((r, h)) * ROWS


def layer_norm(tokens, modulation):
    tokens = tokens.astype(F32)
    centred = tokens - jnp.mean(tokens, axis=1, keepdims=True)
    scaled = centred * lax.rsqrt(jnp.mean(centred * centred, axis=1, keepdims=True) + EPS)
    return (scaled * (1.0 + modulation[1:2]) + modulation[0:1]).astype(BF16)


def head_norm(features, gain):
    normed = features * lax.rsqrt(jnp.mean(features * features, axis=1, keepdims=True) + EPS)
    return (normed * gain).astype(BF16)


def arrived(ref, sem):
    pltpu.make_async_copy(ref, ref, sem).wait()


def kernel(
    img_in, txt_in, imod_in, tmod_in, wp_in, wt_in, wm_in, wtm_in, gains_in,
    out_i, out_t,
    img, txt, imod, tmod, wt, wtm, gains,
    g, gm, wp, w2, kv, kvt, q, tf, tpart, trcv, best_s, total_s, acc_s, o, ox, to, top, tor, rr, rl, sr, sl,
    local_sem, a_send, a_recv, z_send, z_recv, x_send, x_recv,
    tp_send, tp_recv, tk_send, tk_recv, to_send, to_recv, tm_send, tm_recv, far_in,
    w_send, w_recv, o_send, o_recv, r_send, r_recv,
):
    ctx, tp, dp = lax.axis_index("ctx"), lax.axis_index("tp"), lax.axis_index("dp")
    x, z = lax.rem(ctx, NX), lax.div(ctx, NX)
    y, hi = lax.rem(tp, NY), lax.div(tp, NY)
    mirror_ctx = (NZ - 1 - z) * NX + x
    mirror = {"ctx": mirror_ctx, "tp": lax.rem(tp + NY, NTP)}
    far = {"tp": lax.rem(tp + NY, NTP)}
    y_left = {"tp": hi * NY + lax.rem(y + NY - 1, NY)}
    y_right = {"tp": hi * NY + lax.rem(y + 1, NY)}
    x_left = {"ctx": z * NX + lax.rem(x + NX - 1, NX)}
    x_right = {"ctx": z * NX + lax.rem(x + 1, NX)}
    x_opposite = {"ctx": z * NX + lax.rem(x + 2, NX)}
    other_core = {"dp": 1 - dp}
    def start(src, dst, ss, rs, device):
        pltpu.make_async_remote_copy(
            src_ref=src, dst_ref=dst, send_sem=ss, recv_sem=rs,
            device_id=device, device_id_type=pl.DeviceIdType.MESH,
        ).start()

    def ctx_peers(act):
        def step(i, carry):
            act(lax.rem(ctx + i, NCTX))
            return carry

        lax.fori_loop(1, NCTX, step, 0)

    barrier = pltpu.get_barrier_semaphore()

    def greet(device):
        pl.semaphore_signal(barrier, inc=1, device_id=device, device_id_type=pl.DeviceIdType.MESH)

    greet(mirror)
    greet(far)
    ctx_peers(lambda i: greet({"ctx": i}))
    for i in range(1, NY):
        greet({"tp": hi * NY + lax.rem(y + i, NY)})
    greet(other_core)

    loads = []
    wanted = (
        (img_in, img), (txt_in, txt), (imod_in, imod), (tmod_in, tmod), (gains_in, gains),
        (wp_in, wp), (wt_in, wt.at[pl.ds(0, 192)]), (wm_in, w2.at[pl.ds(0, HEAD_DIM)]), (wtm_in, wtm),
    )
    for i, (src, dst) in enumerate(wanted):
        loads.append(pltpu.make_async_copy(src, dst, local_sem.at[i]))
        loads[-1].start()
    for i in range(4):
        loads[i].wait()
    wt[192:256, :] = jnp.zeros((64, 384), BF16)

    normed = layer_norm(img[...], imod[...])
    g[0:ROWS, 0:D] = normed
    gm[:, 0:D] = normed
    tf[...] = layer_norm(txt[...], tmod[...]).astype(F32)

    def columns_of(ref, rows, who):
        base = pl.multiple_of(lax.div(who * 3, 2) * 128, 128)
        wide = ref[rows, pl.ds(base, 256)]
        return jnp.where(lax.rem(who, 2) == 1, pltpu.roll(wide, 192, 1), wide)

    for ref, who in ((g, ctx), (gm, mirror_ctx)):
        columns = columns_of(tf, slice(0, TROWS), who).astype(BF16)
        ref[0:16, D:DW] = columns[:, 0:128]
        ref[16:32, D:DW] = columns[:, 128:256]

    pl.semaphore_wait(barrier, (NCTX - 1) + (NY - 1) + 3)
    pl.semaphore_signal(far_in, inc=1, device_id=far, device_id_type=pl.DeviceIdType.MESH)

    def rows_of(r, h, p):
        return g.at[pl.ds(offset(r, h) + p * 16, 16)]

    def forward(r, h, side, p):
        there = r + 1 if side == 0 else (r + NY - 1) % NY
        if there == 4 and p != side:
            return
        start(
            rows_of(r, h, p), rows_of(there, h, p), a_send, a_recv.at[there, h, p],
            y_left if side == 0 else y_right,
        )

    for p in (0, 1):
        start(gm.at[pl.ds(p * 16, 16)], rows_of(0, 1, p), a_send, a_recv.at[0, 1, p], mirror)
        forward(0, 0, 0, p)
        forward(0, 0, 1, p)

    def tokens(r, h, p):
        if r == 0:
            arrived(rows_of(0, h, p), a_recv.at[0, h, p])
            forward(0, h, 0, p)
            forward(0, h, 1, p)
        elif r == 4:
            arrived(rows_of(4, h, p), a_recv.at[4, h, p])
        else:
            arrived(rows_of(r, h, p), a_recv.at[r, h, p])
            forward(r, h, 0, p)
            arrived(rows_of(NY - r, h, p), a_recv.at[NY - r, h, p])
            forward(NY - r, h, 1, p)

    def gain(i):
        return gains[i : i + 1, :]

    def project(c):
        rows = pl.ds(START[c], COUNT[c])
        out = jnp.dot(g[rows, 0:D], wp[...], preferred_element_type=F32)
        q[rows, :] = head_norm(out[:, 0:128], gain(0))
        kv[0, rows, 0:128] = head_norm(out[:, 128:256], gain(1))
        kv[0, rows, 128:256] = out[:, 256:384].astype(BF16)

    def text_project(c):
        blocks = COUNT[c] // ROWS
        columns = g[pl.ds(START[c], COUNT[c]), D:DW].reshape(blocks, 2, 16, 128)
        columns = jnp.concatenate([columns[:, 0], columns[:, 1]], axis=2).reshape(blocks * 16, 256)
        out = jnp.dot(columns, wt[...], preferred_element_type=F32)
        for b, (r, h) in enumerate(CHUNKS[c]):
            slot = r * 2 + h
            tpart[slot] = out[b * 16 : b * 16 + 16].astype(BF16)
            target = lax.rem(h + hi, 2) * NY + lax.rem(y + r, NY)

            @pl.when(target != ctx)
            def _():
                start(tpart.at[slot], trcv.at[ctx], tp_send, tp_recv, {"ctx": target})

    def kv_rows(k, r, c, part=None):
        count = COUNT[c] if part is None else COUNT[c] // 2
        return kv.at[k * NX + r, pl.ds(START[c] + (0 if part is None else part * count), count)]

    def send_x(c, k):
        start(kv_rows(k, 0, c), kv_rows(k, 1, c), x_send, x_recv.at[c, k, 0], x_left)
        start(kv_rows(k, 0, c), kv_rows(k, 3, c), x_send, x_recv.at[c, k, 1], x_right)
        if c == NCH - 1:
            start(kv_rows(k, 0, c), kv_rows(k, 2, c), x_send, x_recv.at[c, k, 2], x_opposite)

    def spread(c):
        for k in (1, 3, 2):
            device = {"ctx": lax.rem(z + k, NZ) * NX + x}
            start(kv_rows(0, 0, c), kv_rows(NZ - k, 0, c), z_send, z_recv.at[c, NZ - k], device)
        send_x(c, 0)

    def across(c, k):
        arrived(kv_rows(k, 0, c), z_recv.at[c, k])
        send_x(c, k)

    def around(c, k):
        arrived(kv_rows(k, 1, c), x_recv.at[c, k, 0])
        if c == NCH - 1:
            arrived(kv_rows(k, 3, c), x_recv.at[c, k, 1])
            return
        start(kv_rows(k, 1, c, 0), kv_rows(k, 2, c, 0), x_send, x_recv.at[c, k, 2], x_left)
        arrived(kv_rows(k, 3, c), x_recv.at[c, k, 1])
        start(kv_rows(k, 3, c, 1), kv_rows(k, 2, c, 1), x_send, x_recv.at[c, k, 2], x_right)

    def complete(c):
        for k in range(NZ):
            arrived(kv_rows(k, 2, c), x_recv.at[c, k, 2])

    def merge_half(core):
        return w2.at[pl.ds(pl.multiple_of(HEAD_DIM + core * 64, 64), 64)]

    def merge_weights(step):
        if step == 0:
            loads[7].wait()
            start(w2.at[pl.ds(pl.multiple_of(dp * 64, 64), 64)], merge_half(dp), w_send, w_recv.at[0], mirror)
        elif step == 1:
            arrived(merge_half(dp), w_recv.at[0])
            start(merge_half(dp), merge_half(dp), w_send, w_recv.at[1], other_core)
        else:
            arrived(merge_half(1 - dp), w_recv.at[1])

    def text_rows(i):
        return kvt.at[pl.ds(pl.multiple_of(i * TROWS, TROWS), TROWS)]

    def text_heads():
        arrived(trcv.at[pl.ds(0, NCTX - 1)], tp_recv)
        own = lax.rem(lax.rem(ctx, NY) + NY - y, NY) * 2 + lax.rem(lax.div(ctx, NY) + hi, 2)
        trcv[ctx] = tpart[own]
        total = jnp.sum(trcv[...].astype(F32), axis=0)
        q[512:NQ, :] = head_norm(total[:, 0:128], gain(2))
        mine = pl.ds(pl.multiple_of(ctx * TROWS, TROWS), TROWS)
        kvt[mine, 0:128] = head_norm(total[:, 128:256], gain(3))
        kvt[mine, 128:256] = total[:, 256:384].astype(BF16)
        ctx_peers(lambda i: start(text_rows(ctx), text_rows(ctx), tk_send, tk_recv, {"ctx": i}))

    scale = HEAD_DIM**-0.5 * LOG2E

    def fold(state, query, key_blocks):
        best, total, weighted = state
        for both in key_blocks:
            s = lax.dot_general(query, both[:, 0:128], (((1,), (1,)), ((), ())), preferred_element_type=F32)
            fresh = jnp.maximum(best, jnp.max(s, axis=1, keepdims=True))
            decay = jnp.exp2((best - fresh) * scale)
            weights = jnp.exp2((s - fresh) * scale)
            total = total * decay + jnp.sum(weights, axis=1, keepdims=True)
            weighted = weighted * decay + jnp.dot(weights.astype(BF16), both[:, 128:256], preferred_element_type=F32)
            best = fresh
        return best, total, weighted

    def attend(first, end, low, high):
        rows = pl.ds(first, end - first)
        count = START[high] + COUNT[high] - START[low]
        both = kv[:, pl.ds(START[low], count)].reshape(NCTX * count, 256)
        state = fold((best_s[rows, :], total_s[rows, :], acc_s[rows, :]), q[rows, :], [both])
        best_s[rows, :], total_s[rows, :], acc_s[rows, :] = state

    def finish(c, low):
        first = RING[c][0]
        ranges = [(offset(first, h), RCOUNT[c]) for h in (0, 1)]
        if c == 4:
            ranges.append((512, TROWS))

        def rows_from(ref):
            return jnp.concatenate([ref[pl.ds(at, n), :] for at, n in ranges], axis=0)

        count = START[-1] + COUNT[-1] - START[low]
        last = kv[:, pl.ds(START[low], count)].reshape(NCTX * count, 256)
        state = (rows_from(best_s), rows_from(total_s), rows_from(acc_s))
        best, total, weighted = fold(state, rows_from(q), [last, kvt[...]])
        return (weighted / total).astype(BF16)

    best_s[...] = jnp.full((NQ, 1), -1e30, F32)
    total_s[...] = jnp.zeros((NQ, 1), F32)
    acc_s[...] = jnp.zeros((NQ, HEAD_DIM), F32)

    def enter(c):
        text_project(c)
        project(c)
        spread(c)

    tokens(1, 0, 0)
    tokens(1, 0, 1)
    for i in (4, 5, 6):
        loads[i].wait()
    enter(0)
    tokens(2, 0, 0)
    tokens(0, 1, 0)
    around(0, 0)
    tokens(2, 0, 1)
    enter(1)
    tokens(0, 1, 1)
    merge_weights(0)
    across(0, 3)
    tokens(3, 0, 0)
    across(0, 1)
    around(1, 0)
    across(0, 2)
    tokens(1, 1, 0)
    around(0, 3)
    across(1, 3)
    around(0, 1)
    tokens(3, 0, 1)
    enter(2)
    around(0, 2)
    across(1, 1)
    across(1, 2)
    tokens(1, 1, 1)
    enter(3)
    around(1, 3)
    tokens(4, 0, 0)
    tokens(4, 0, 1)
    around(2, 0)
    complete(0)
    across(2, 3)
    around(1, 1)
    tokens(2, 1, 0)
    around(1, 2)
    across(2, 1)
    around(3, 0)
    across(2, 2)
    tokens(2, 1, 1)
    enter(4)
    around(2, 3)
    across(3, 3)
    complete(1)
    attend(0, 256, 0, 1)
    tokens(3, 1, 0)
    around(2, 1)
    across(3, 1)
    across(3, 2)
    around(2, 2)
    tokens(3, 1, 1)
    enter(5)
    around(3, 3)
    around(4, 0)
    across(4, 3)
    around(3, 1)
    across(4, 1)
    merge_weights(1)
    around(3, 2)
    tokens(4, 1, 0)
    tokens(4, 1, 1)
    enter(6)
    around(5, 0)
    across(4, 2)
    complete(2)
    attend(256, 512, 0, 1)
    across(5, 3)
    around(4, 3)
    across(5, 1)
    across(5, 2)
    around(4, 1)
    complete(3)
    attend(0, 256, 2, 3)
    around(6, 0)
    across(6, 1)
    across(6, 3)
    across(6, 2)
    attend(256, 512, 2, 3)
    text_heads()
    around(4, 2)
    around(5, 1)
    around(5, 3)
    attend(512, 528, 0, 3)
    around(5, 2)
    around(6, 1)
    around(6, 3)
    around(6, 2)
    complete(4)
    complete(6)
    complete(5)
    arrived(kvt.at[pl.ds(0, (NCTX - 1) * TROWS)], tk_recv)
    merge_weights(2)

    def exchange(c, low=NCH - 1):
        half = RCOUNT[c]
        rows = pl.ds(RSTART[c], half)
        mixed = finish(c, low)
        ox[rows, :] = mixed[half : 2 * half]
        start(ox.at[rows], o.at[rows, pl.ds(128, 128)], o_send, o_recv.at[c], mirror)
        o[rows, 0:128] = mixed[0:half]
        if c == 4:
            to[ctx] = mixed[2 * half :]
            ctx_peers(lambda i: start(to.at[ctx], to.at[ctx], to_send, to_recv, {"ctx": i}))

    def text_merge(step):
        if step == 0:
            arrived(to.at[pl.ds(0, NCTX - 1)], to_recv)
            loads[8].wait()
            part = lax.dot_general(
                to[...].reshape(NCTX * TROWS, HEAD_DIM), wtm[...], (((1,), (1,)), ((), ())), preferred_element_type=F32
            )
            top[:, :, 0:192] = part.reshape(NTP, TROWS, 192).astype(BF16)
            top[:, :, 192:256] = jnp.zeros((NTP, TROWS, 64), BF16)
            pl.semaphore_wait(far_in, 1)

            def step(i, carry):
                there = lax.rem(tp + i, NTP)
                start(top.at[there], tor.at[i], tm_send, tm_recv, {"tp": there})
                return carry

            lax.fori_loop(1, NTP, step, 0)
        else:
            arrived(tor.at[pl.ds(1, NTP - 1)], tm_recv)
            tor[0] = top[tp]
            text_total = jnp.sum(tor[...].astype(F32), axis=0)[:, 0:192]
            tf[0:3, :] = tmod[...]
            gate = columns_of(tf, slice(2, 3), ctx)[:, 0:192]
            out_t[...] = (gate * text_total).astype(BF16)

    def merge(c):
        rows = pl.ds(RSTART[c], RCOUNT[c])
        arrived(o.at[rows, pl.ds(128, 128)], o_recv.at[c])
        return jnp.dot(o[rows, :], w2[...], preferred_element_type=F32)

    def reduce(c):
        part = merge(c)
        for turn in (0, 1):
            for j in (0, 1):
                columns = slice(j * HALF, j * HALF + HALF)
                if c == 0:
                    p = turn
                    half, ref = slice(p * 16, p * 16 + 16), pl.ds(p * 16, 16)
                    for way, recv in enumerate((rr, rl)):
                        arrived(recv.at[0, j, ref], r_recv.at[way, 0, p, j])
                    sums = part[half, columns] + rr[0, j, half, :].astype(F32) + rl[0, j, half, :].astype(F32)
                    out_i[half, columns] = (imod[2:3, columns] * sums).astype(BF16)
                    continue
                for way, recv, out, device in ((0, rr, sr, y_right), (1, rl, sl, y_left)):
                    p = 1 - way if turn == 0 else way
                    half, ref = slice(p * 16, p * 16 + 16), pl.ds(p * 16, 16)
                    if c == 4:
                        if p != way:
                            continue
                        sums = part[half, columns]
                    else:
                        first = way * ROWS + p * 16
                        sums = part[first : first + 16, columns]
                        if c < 3 or p == way:
                            arrived(recv.at[c, j, ref], r_recv.at[way, c, p, j])
                            sums = sums + recv[c, j, half, :].astype(F32)
                    out[c - 1, j, half, :] = sums.astype(BF16)
                    start(out.at[c - 1, j, ref], recv.at[c - 1, j, ref], r_send, r_recv.at[way, c - 1, p, j], device)

    exchange(4, 4)
    attend(0, 528, 4, NCH - 2)
    exchange(3)
    reduce(4)
    exchange(2)
    text_merge(0)
    reduce(3)
    exchange(1)
    reduce(2)
    exchange(0)
    reduce(1)
    text_merge(1)
    reduce(0)

    arrived(g.at[pl.ds(0, 480)], a_send)
    arrived(kv.at[pl.ds(0, 3)], z_send)
    arrived(kv.at[pl.ds(0, 12)], x_send)
    arrived(tpart.at[pl.ds(0, NCTX - 1)], tp_send)
    arrived(kvt.at[pl.ds(0, (NCTX - 1) * TROWS)], tk_send)
    arrived(to.at[pl.ds(0, NCTX - 1)], to_send)
    arrived(tor.at[pl.ds(0, NTP - 1)], tm_send)
    arrived(w2.at[pl.ds(0, 128)], w_send)
    arrived(ox, o_send)
    arrived(w2.at[pl.ds(0, 224)], r_send)


def on_device(*arrays):
    arrays = arrays[:7] + (arrays[7].T,) + arrays[8:]
    dma = pltpu.SemaphoreType.DMA
    vmem = pl.BlockSpec(memory_space=pltpu.VMEM)
    hbm = pl.BlockSpec(memory_space=pltpu.HBM)
    return pl.pallas_call(
        kernel,
        out_shape=(
            jax.ShapeDtypeStruct((ROWS, D), BF16),
            jax.ShapeDtypeStruct((TROWS, 192), BF16),
        ),
        in_specs=[hbm] * 9,
        out_specs=(vmem, vmem),
        scratch_shapes=[
            pltpu.VMEM((ROWS, D), BF16),
            pltpu.VMEM((TROWS, D), BF16),
            pltpu.VMEM((3, D), F32),
            pltpu.VMEM((3, D), F32),
            pltpu.VMEM((256, 384), BF16),
            pltpu.VMEM((192, HEAD_DIM), BF16),
            pltpu.VMEM((4, HEAD_DIM), F32),
            pltpu.VMEM((512, DW), BF16),
            pltpu.VMEM((ROWS, DW), BF16),
            pltpu.VMEM((D, 384), BF16),
            pltpu.VMEM((256, D), BF16),
            pltpu.VMEM((NCTX, 512, 256), BF16),
            pltpu.VMEM((NCTX * TROWS, 256), BF16),
            pltpu.VMEM((NQ, HEAD_DIM), BF16),
            pltpu.VMEM((TROWS, D), F32),
            pltpu.VMEM((NTP, TROWS, 384), BF16),
            pltpu.VMEM((NCTX, TROWS, 384), BF16),
            pltpu.VMEM((NQ, 1), F32),
            pltpu.VMEM((NQ, 1), F32),
            pltpu.VMEM((NQ, HEAD_DIM), F32),
            pltpu.VMEM((256, 256), BF16),
            pltpu.VMEM((256, HEAD_DIM), BF16),
            pltpu.VMEM((NCTX, TROWS, HEAD_DIM), BF16),
            pltpu.VMEM((NTP, TROWS, 256), BF16),
            pltpu.VMEM((NTP, TROWS, 256), BF16),
            pltpu.VMEM((4, 2, ROWS, HALF), BF16),
            pltpu.VMEM((4, 2, ROWS, HALF), BF16),
            pltpu.VMEM((4, 2, ROWS, HALF), BF16),
            pltpu.VMEM((4, 2, ROWS, HALF), BF16),
            dma((9,)),
            dma,
            dma((NY, 2, 2)),
            dma,
            dma((NCH, NZ)),
            dma,
            dma((NCH, NZ, 3)),
            dma, dma,
            dma, dma,
            dma, dma,
            dma, dma,
            pltpu.SemaphoreType.REGULAR,
            dma, dma((2,)),
            dma, dma((5,)),
            dma, dma((2, 4, 2, 2)),
        ],
        compiler_params=pltpu.CompilerParams(
            collective_id=0, has_side_effects=True, vmem_limit_bytes=63 * 1024 * 1024
        ),
        cost_estimate=pl.CostEstimate(flops=7_000_000_000, bytes_accessed=8_000_000, transcendentals=4_500_000),
        name="joint_attention",
    )(*arrays)


def solution(mesh):
    placed = (
        P(("dp", "ctx", "tp"), None),
        P(("dp", "tp"), None),
        P("dp", None),
        P("dp", None),
        P(None, "tp"),
        P("ctx", "tp"),
        P("tp", None),
        P("tp", "ctx"),
        P(),
    )
    return jax.shard_map(
        on_device,
        mesh=mesh,
        in_specs=placed,
        out_specs=(P(("dp", "ctx", "tp"), None), P(("dp", "tp"), "ctx")),
        check_vma=False,
    )
```

```python
import jax
import jax.numpy as jnp
from jax import lax
from jax.experimental import pallas as pl
from jax.experimental.pallas import tpu as pltpu
from jax.sharding import PartitionSpec as P

HEAD_DIM = 128
D = 3072
EPS = 1e-06
HALF = D // 2
DW = D + 128
NX, NZ, NY, NCTX, NTP = 4, 4, 8, 16, 16
ROWS = 32
TROWS = 16
CHUNKS = (
    ((0, 0), (1, 0), (7, 0)),
    ((2, 0), (6, 0)),
    ((0, 1), (3, 0), (5, 0)),
    ((1, 1), (7, 1)),
    ((4, 0), (2, 1), (6, 1)),
    ((3, 1), (5, 1)),
    ((4, 1),),
)
COUNT = tuple(32 * len(members) for members in CHUNKS)
START = tuple(sum(COUNT[:c]) for c in range(len(CHUNKS)))
NCH = len(CHUNKS)
RING = ((0,), (1, 7), (2, 6), (3, 5), (4,))
RSTART = (0, 32, 96, 160, 224)
RCOUNT = (32, 64, 64, 64, 32)
NQ = 512 + TROWS
F32, BF16 = jnp.float32, jnp.bfloat16
LOG2E = 1.4426950408889634


def offset(r, h):
    for c, members in enumerate(CHUNKS):
        if (r, h) in members:
            return START[c] + members.index((r, h)) * ROWS


def layer_norm(tokens, modulation):
    tokens = tokens.astype(F32)
    centred = tokens - jnp.mean(tokens, axis=1, keepdims=True)
    scaled = centred * lax.rsqrt(jnp.mean(centred * centred, axis=1, keepdims=True) + EPS)
    return (scaled * (1.0 + modulation[1:2]) + modulation[0:1]).astype(BF16)


def head_norm(features, gain):
    normed = features * lax.rsqrt(jnp.mean(features * features, axis=1, keepdims=True) + EPS)
    return (normed * gain).astype(BF16)


def arrived(ref, sem):
    pltpu.make_async_copy(ref, ref, sem).wait()


def kernel(
    img_in, txt_in, imod_in, tmod_in, wp_in, wt_in, wm_in, wtm_in, gains_in,
    out_i, out_t,
    img, txt, imod, tmod, wt, wtm, gains,
    g, gm, wp, w2, kv, kvt, q, tf, tpart, trcv, best_s, total_s, acc_s, o, ox, to, top, tor, rr, rl, sr, sl,
    local_sem, a_send, a_recv, z_send, z_recv, x_send, x_recv,
    tp_send, tp_recv, tk_send, tk_recv, to_send, to_recv, tm_send, tm_recv, far_in,
    w_send, w_recv, o_send, o_recv, r_send, r_recv,
):
    ctx, tp, dp = lax.axis_index("ctx"), lax.axis_index("tp"), lax.axis_index("dp")
    x, z = lax.rem(ctx, NX), lax.div(ctx, NX)
    y, hi = lax.rem(tp, NY), lax.div(tp, NY)
    mirror_ctx = (NZ - 1 - z) * NX + x
    mirror = {"ctx": mirror_ctx, "tp": lax.rem(tp + NY, NTP)}
    far = {"tp": lax.rem(tp + NY, NTP)}
    y_left = {"tp": hi * NY + lax.rem(y + NY - 1, NY)}
    y_right = {"tp": hi * NY + lax.rem(y + 1, NY)}
    x_left = {"ctx": z * NX + lax.rem(x + NX - 1, NX)}
    x_right = {"ctx": z * NX + lax.rem(x + 1, NX)}
    x_opposite = {"ctx": z * NX + lax.rem(x + 2, NX)}
    other_core = {"dp": 1 - dp}
    def start(src, dst, ss, rs, device):
        pltpu.make_async_remote_copy(
            src_ref=src, dst_ref=dst, send_sem=ss, recv_sem=rs,
            device_id=device, device_id_type=pl.DeviceIdType.MESH,
        ).start()

    def ctx_peers(act):
        def step(i, carry):
            act(lax.rem(ctx + i, NCTX))
            return carry

        lax.fori_loop(1, NCTX, step, 0)

    barrier = pltpu.get_barrier_semaphore()

    def greet(device):
        pl.semaphore_signal(barrier, inc=1, device_id=device, device_id_type=pl.DeviceIdType.MESH)

    greet(mirror)
    greet(far)
    ctx_peers(lambda i: greet({"ctx": i}))
    for i in range(1, NY):
        greet({"tp": hi * NY + lax.rem(y + i, NY)})
    greet(other_core)

    loads = []
    wanted = (
        (img_in, img), (txt_in, txt), (imod_in, imod), (tmod_in, tmod), (gains_in, gains),
        (wp_in, wp), (wt_in, wt.at[pl.ds(0, 192)]), (wm_in, w2.at[pl.ds(0, HEAD_DIM)]), (wtm_in, wtm),
    )
    for i, (src, dst) in enumerate(wanted):
        loads.append(pltpu.make_async_copy(src, dst, local_sem.at[i]))
        loads[-1].start()
    for i in range(4):
        loads[i].wait()
    wt[192:256, :] = jnp.zeros((64, 384), BF16)

    normed = layer_norm(img[...], imod[...])
    g[0:ROWS, 0:D] = normed
    gm[:, 0:D] = normed
    tf[...] = layer_norm(txt[...], tmod[...]).astype(F32)

    def columns_of(ref, rows, who):
        base = pl.multiple_of(lax.div(who * 3, 2) * 128, 128)
        wide = ref[rows, pl.ds(base, 256)]
        return jnp.where(lax.rem(who, 2) == 1, pltpu.roll(wide, 192, 1), wide)

    for ref, who in ((g, ctx), (gm, mirror_ctx)):
        columns = columns_of(tf, slice(0, TROWS), who).astype(BF16)
        ref[0:16, D:DW] = columns[:, 0:128]
        ref[16:32, D:DW] = columns[:, 128:256]

    pl.semaphore_wait(barrier, (NCTX - 1) + (NY - 1) + 3)
    pl.semaphore_signal(far_in, inc=1, device_id=far, device_id_type=pl.DeviceIdType.MESH)

    def rows_of(r, h, p):
        return g.at[pl.ds(offset(r, h) + p * 16, 16)]

    def forward(r, h, side, p):
        there = r + 1 if side == 0 else (r + NY - 1) % NY
        if there == 4 and p != side:
            return
        start(
            rows_of(r, h, p), rows_of(there, h, p), a_send, a_recv.at[there, h, p],
            y_left if side == 0 else y_right,
        )

    for p in (0, 1):
        start(gm.at[pl.ds(p * 16, 16)], rows_of(0, 1, p), a_send, a_recv.at[0, 1, p], mirror)
        forward(0, 0, 0, p)
        forward(0, 0, 1, p)

    def tokens(r, h, p):
        if r == 0:
            arrived(rows_of(0, h, p), a_recv.at[0, h, p])
            forward(0, h, 0, p)
            forward(0, h, 1, p)
        elif r == 4:
            arrived(rows_of(4, h, p), a_recv.at[4, h, p])
        else:
            arrived(rows_of(r, h, p), a_recv.at[r, h, p])
            forward(r, h, 0, p)
            arrived(rows_of(NY - r, h, p), a_recv.at[NY - r, h, p])
            forward(NY - r, h, 1, p)

    def gain(i):
        return gains[i : i + 1, :]

    def project(c):
        rows = pl.ds(START[c], COUNT[c])
        out = jnp.dot(g[rows, 0:D], wp[...], preferred_element_type=F32)
        q[rows, :] = head_norm(out[:, 0:128], gain(0))
        kv[0, rows, 0:128] = head_norm(out[:, 128:256], gain(1))
        kv[0, rows, 128:256] = out[:, 256:384].astype(BF16)

    def text_project(c):
        blocks = COUNT[c] // ROWS
        columns = g[pl.ds(START[c], COUNT[c]), D:DW].reshape(blocks, 2, 16, 128)
        columns = jnp.concatenate([columns[:, 0], columns[:, 1]], axis=2).reshape(blocks * 16, 256)
        out = jnp.dot(columns, wt[...], preferred_element_type=F32)
        for b, (r, h) in enumerate(CHUNKS[c]):
            slot = r * 2 + h
            tpart[slot] = out[b * 16 : b * 16 + 16].astype(BF16)
            target = lax.rem(h + hi, 2) * NY + lax.rem(y + r, NY)

            @pl.when(target != ctx)
            def _():
                start(tpart.at[slot], trcv.at[ctx], tp_send, tp_recv, {"ctx": target})

    def kv_rows(k, r, c, part=None):
        count = COUNT[c] if part is None else COUNT[c] // 2
        return kv.at[k * NX + r, pl.ds(START[c] + (0 if part is None else part * count), count)]

    def send_x(c, k):
        start(kv_rows(k, 0, c), kv_rows(k, 1, c), x_send, x_recv.at[c, k, 0], x_left)
        start(kv_rows(k, 0, c), kv_rows(k, 3, c), x_send, x_recv.at[c, k, 1], x_right)
        if c == NCH - 1:
            start(kv_rows(k, 0, c), kv_rows(k, 2, c), x_send, x_recv.at[c, k, 2], x_opposite)

    def spread(c):
        for k in (1, 3, 2):
            device = {"ctx": lax.rem(z + k, NZ) * NX + x}
            start(kv_rows(0, 0, c), kv_rows(NZ - k, 0, c), z_send, z_recv.at[c, NZ - k], device)
        send_x(c, 0)

    def across(c, k):
        arrived(kv_rows(k, 0, c), z_recv.at[c, k])
        send_x(c, k)

    def around(c, k):
        arrived(kv_rows(k, 1, c), x_recv.at[c, k, 0])
        if c == NCH - 1:
            arrived(kv_rows(k, 3, c), x_recv.at[c, k, 1])
            return
        start(kv_rows(k, 1, c, 0), kv_rows(k, 2, c, 0), x_send, x_recv.at[c, k, 2], x_left)
        arrived(kv_rows(k, 3, c), x_recv.at[c, k, 1])
        start(kv_rows(k, 3, c, 1), kv_rows(k, 2, c, 1), x_send, x_recv.at[c, k, 2], x_right)

    def complete(c):
        for k in range(NZ):
            arrived(kv_rows(k, 2, c), x_recv.at[c, k, 2])

    def merge_half(core):
        return w2.at[pl.ds(pl.multiple_of(HEAD_DIM + core * 64, 64), 64)]

    def merge_weights(step):
        if step == 0:
            loads[7].wait()
            start(w2.at[pl.ds(pl.multiple_of(dp * 64, 64), 64)], merge_half(dp), w_send, w_recv.at[0], mirror)
        elif step == 1:
            arrived(merge_half(dp), w_recv.at[0])
            start(merge_half(dp), merge_half(dp), w_send, w_recv.at[1], other_core)
        else:
            arrived(merge_half(1 - dp), w_recv.at[1])

    def text_rows(i):
        return kvt.at[pl.ds(pl.multiple_of(i * TROWS, TROWS), TROWS)]

    def text_heads():
        arrived(trcv.at[pl.ds(0, NCTX - 1)], tp_recv)
        own = lax.rem(lax.rem(ctx, NY) + NY - y, NY) * 2 + lax.rem(lax.div(ctx, NY) + hi, 2)
        trcv[ctx] = tpart[own]
        total = jnp.sum(trcv[...].astype(F32), axis=0)
        q[512:NQ, :] = head_norm(total[:, 0:128], gain(2))
        mine = pl.ds(pl.multiple_of(ctx * TROWS, TROWS), TROWS)
        kvt[mine, 0:128] = head_norm(total[:, 128:256], gain(3))
        kvt[mine, 128:256] = total[:, 256:384].astype(BF16)
        ctx_peers(lambda i: start(text_rows(ctx), text_rows(ctx), tk_send, tk_recv, {"ctx": i}))

    scale = HEAD_DIM**-0.5 * LOG2E

    def fold(state, query, key_blocks):
        best, total, weighted = state
        for both in key_blocks:
            s = lax.dot_general(query, both[:, 0:128], (((1,), (1,)), ((), ())), preferred_element_type=F32)
            fresh = jnp.maximum(best, jnp.max(s, axis=1, keepdims=True))
            decay = jnp.exp2((best - fresh) * scale)
            weights = jnp.exp2((s - fresh) * scale)
            total = total * decay + jnp.sum(weights, axis=1, keepdims=True)
            weighted = weighted * decay + jnp.dot(weights.astype(BF16), both[:, 128:256], preferred_element_type=F32)
            best = fresh
        return best, total, weighted

    def attend(first, end, low, high):
        rows = pl.ds(first, end - first)
        count = START[high] + COUNT[high] - START[low]
        both = kv[:, pl.ds(START[low], count)].reshape(NCTX * count, 256)
        state = fold((best_s[rows, :], total_s[rows, :], acc_s[rows, :]), q[rows, :], [both])
        best_s[rows, :], total_s[rows, :], acc_s[rows, :] = state

    def finish(c, low):
        first = RING[c][0]
        ranges = [(offset(first, h), RCOUNT[c]) for h in (0, 1)]
        if c == 4:
            ranges.append((512, TROWS))

        def rows_from(ref):
            return jnp.concatenate([ref[pl.ds(at, n), :] for at, n in ranges], axis=0)

        count = START[-1] + COUNT[-1] - START[low]
        last = kv[:, pl.ds(START[low], count)].reshape(NCTX * count, 256)
        state = (rows_from(best_s), rows_from(total_s), rows_from(acc_s))
        best, total, weighted = fold(state, rows_from(q), [last, kvt[...]])
        return (weighted / total).astype(BF16)

    best_s[...] = jnp.full((NQ, 1), -1e30, F32)
    total_s[...] = jnp.zeros((NQ, 1), F32)
    acc_s[...] = jnp.zeros((NQ, HEAD_DIM), F32)

    def enter(c):
        text_project(c)
        project(c)
        spread(c)

    tokens(1, 0, 0)
    tokens(1, 0, 1)
    for i in (4, 5, 6):
        loads[i].wait()
    enter(0)
    tokens(2, 0, 0)
    tokens(0, 1, 0)
    around(0, 0)
    tokens(2, 0, 1)
    enter(1)
    tokens(0, 1, 1)
    merge_weights(0)
    across(0, 3)
    tokens(3, 0, 0)
    across(0, 1)
    around(1, 0)
    across(0, 2)
    tokens(1, 1, 0)
    around(0, 3)
    across(1, 3)
    around(0, 1)
    tokens(3, 0, 1)
    enter(2)
    around(0, 2)
    across(1, 1)
    across(1, 2)
    tokens(1, 1, 1)
    enter(3)
    around(1, 3)
    tokens(4, 0, 0)
    tokens(4, 0, 1)
    around(2, 0)
    complete(0)
    across(2, 3)
    around(1, 1)
    tokens(2, 1, 0)
    around(1, 2)
    across(2, 1)
    around(3, 0)
    across(2, 2)
    tokens(2, 1, 1)
    enter(4)
    around(2, 3)
    across(3, 3)
    complete(1)
    attend(0, 256, 0, 1)
    tokens(3, 1, 0)
    around(2, 1)
    across(3, 1)
    across(3, 2)
    around(2, 2)
    tokens(3, 1, 1)
    enter(5)
    around(3, 3)
    around(4, 0)
    across(4, 3)
    around(3, 1)
    across(4, 1)
    merge_weights(1)
    around(3, 2)
    tokens(4, 1, 0)
    tokens(4, 1, 1)
    enter(6)
    around(5, 0)
    across(4, 2)
    complete(2)
    attend(256, 512, 0, 1)
    across(5, 3)
    around(4, 3)
    across(5, 1)
    across(5, 2)
    around(4, 1)
    complete(3)
    text_heads()
    attend(0, 256, 2, 3)
    around(6, 0)
    across(6, 1)
    across(6, 3)
    across(6, 2)
    attend(256, 512, 2, 3)
    around(4, 2)
    around(5, 1)
    around(5, 3)
    attend(512, 528, 0, 3)
    around(5, 2)
    around(6, 1)
    around(6, 3)
    around(6, 2)
    complete(4)
    complete(6)
    complete(5)

    def exchange(c, low=NCH - 1):
        half = RCOUNT[c]
        rows = pl.ds(RSTART[c], half)
        mixed = finish(c, low)
        ox[rows, :] = mixed[half : 2 * half]
        start(ox.at[rows], o.at[rows, pl.ds(128, 128)], o_send, o_recv.at[c], mirror)
        o[rows, 0:128] = mixed[0:half]
        if c == 4:
            to[ctx] = mixed[2 * half :]
            ctx_peers(lambda i: start(to.at[ctx], to.at[ctx], to_send, to_recv, {"ctx": i}))

    def text_merge(step):
        if step == 0:
            arrived(to.at[pl.ds(0, NCTX - 1)], to_recv)
            loads[8].wait()
            part = lax.dot_general(
                to[...].reshape(NCTX * TROWS, HEAD_DIM), wtm[...], (((1,), (1,)), ((), ())), preferred_element_type=F32
            )
            top[:, :, 0:192] = part.reshape(NTP, TROWS, 192).astype(BF16)
            top[:, :, 192:256] = jnp.zeros((NTP, TROWS, 64), BF16)
            pl.semaphore_wait(far_in, 1)

            def step(i, carry):
                there = lax.rem(tp + i, NTP)
                start(top.at[there], tor.at[i], tm_send, tm_recv, {"tp": there})
                return carry

            lax.fori_loop(1, NTP, step, 0)
        else:
            arrived(tor.at[pl.ds(1, NTP - 1)], tm_recv)
            tor[0] = top[tp]
            text_total = jnp.sum(tor[...].astype(F32), axis=0)[:, 0:192]
            tf[0:3, :] = tmod[...]
            gate = columns_of(tf, slice(2, 3), ctx)[:, 0:192]
            out_t[...] = (gate * text_total).astype(BF16)

    def merge(c):
        rows = pl.ds(RSTART[c], RCOUNT[c])
        arrived(o.at[rows, pl.ds(128, 128)], o_recv.at[c])
        return jnp.dot(o[rows, :], w2[...], preferred_element_type=F32)

    def reduce(c):
        part = merge(c)
        for turn in (0, 1):
            for j in (0, 1):
                columns = slice(j * HALF, j * HALF + HALF)
                if c == 0:
                    p = turn
                    half, ref = slice(p * 16, p * 16 + 16), pl.ds(p * 16, 16)
                    for way, recv in enumerate((rr, rl)):
                        arrived(recv.at[0, j, ref], r_recv.at[way, 0, p, j])
                    sums = part[half, columns] + rr[0, j, half, :].astype(F32) + rl[0, j, half, :].astype(F32)
                    out_i[half, columns] = (imod[2:3, columns] * sums).astype(BF16)
                    continue
                for way, recv, out, device in ((0, rr, sr, y_right), (1, rl, sl, y_left)):
                    p = 1 - way if turn == 0 else way
                    half, ref = slice(p * 16, p * 16 + 16), pl.ds(p * 16, 16)
                    if c == 4:
                        if p != way:
                            continue
                        sums = part[half, columns]
                    else:
                        first = way * ROWS + p * 16
                        sums = part[first : first + 16, columns]
                        if c < 3 or p == way:
                            arrived(recv.at[c, j, ref], r_recv.at[way, c, p, j])
                            sums = sums + recv[c, j, half, :].astype(F32)
                    out[c - 1, j, half, :] = sums.astype(BF16)
                    start(out.at[c - 1, j, ref], recv.at[c - 1, j, ref], r_send, r_recv.at[way, c - 1, p, j], device)

    attend(0, 528, 4, NCH - 2)
    arrived(kvt.at[pl.ds(0, (NCTX - 1) * TROWS)], tk_recv)
    merge_weights(2)
    exchange(4)
    exchange(3)
    reduce(4)
    exchange(2)
    text_merge(0)
    reduce(3)
    exchange(1)
    reduce(2)
    exchange(0)
    reduce(1)
    text_merge(1)
    reduce(0)

    arrived(g.at[pl.ds(0, 480)], a_send)
    arrived(kv.at[pl.ds(0, 3)], z_send)
    arrived(kv.at[pl.ds(0, 12)], x_send)
    arrived(tpart.at[pl.ds(0, NCTX - 1)], tp_send)
    arrived(kvt.at[pl.ds(0, (NCTX - 1) * TROWS)], tk_send)
    arrived(to.at[pl.ds(0, NCTX - 1)], to_send)
    arrived(tor.at[pl.ds(0, NTP - 1)], tm_send)
    arrived(w2.at[pl.ds(0, 128)], w_send)
    arrived(ox, o_send)
    arrived(w2.at[pl.ds(0, 224)], r_send)


def on_device(*arrays):
    arrays = arrays[:7] + (arrays[7].T,) + arrays[8:]
    dma = pltpu.SemaphoreType.DMA
    vmem = pl.BlockSpec(memory_space=pltpu.VMEM)
    hbm = pl.BlockSpec(memory_space=pltpu.HBM)
    return pl.pallas_call(
        kernel,
        out_shape=(
            jax.ShapeDtypeStruct((ROWS, D), BF16),
            jax.ShapeDtypeStruct((TROWS, 192), BF16),
        ),
        in_specs=[hbm] * 9,
        out_specs=(vmem, vmem),
        scratch_shapes=[
            pltpu.VMEM((ROWS, D), BF16),
            pltpu.VMEM((TROWS, D), BF16),
            pltpu.VMEM((3, D), F32),
            pltpu.VMEM((3, D), F32),
            pltpu.VMEM((256, 384), BF16),
            pltpu.VMEM((192, HEAD_DIM), BF16),
            pltpu.VMEM((4, HEAD_DIM), F32),
            pltpu.VMEM((512, DW), BF16),
            pltpu.VMEM((ROWS, DW), BF16),
            pltpu.VMEM((D, 384), BF16),
            pltpu.VMEM((256, D), BF16),
            pltpu.VMEM((NCTX, 512, 256), BF16),
            pltpu.VMEM((NCTX * TROWS, 256), BF16),
            pltpu.VMEM((NQ, HEAD_DIM), BF16),
            pltpu.VMEM((TROWS, D), F32),
            pltpu.VMEM((NTP, TROWS, 384), BF16),
            pltpu.VMEM((NCTX, TROWS, 384), BF16),
            pltpu.VMEM((NQ, 1), F32),
            pltpu.VMEM((NQ, 1), F32),
            pltpu.VMEM((NQ, HEAD_DIM), F32),
            pltpu.VMEM((256, 256), BF16),
            pltpu.VMEM((256, HEAD_DIM), BF16),
            pltpu.VMEM((NCTX, TROWS, HEAD_DIM), BF16),
            pltpu.VMEM((NTP, TROWS, 256), BF16),
            pltpu.VMEM((NTP, TROWS, 256), BF16),
            pltpu.VMEM((4, 2, ROWS, HALF), BF16),
            pltpu.VMEM((4, 2, ROWS, HALF), BF16),
            pltpu.VMEM((4, 2, ROWS, HALF), BF16),
            pltpu.VMEM((4, 2, ROWS, HALF), BF16),
            dma((9,)),
            dma,
            dma((NY, 2, 2)),
            dma,
            dma((NCH, NZ)),
            dma,
            dma((NCH, NZ, 3)),
            dma, dma,
            dma, dma,
            dma, dma,
            dma, dma,
            pltpu.SemaphoreType.REGULAR,
            dma, dma((2,)),
            dma, dma((5,)),
            dma, dma((2, 4, 2, 2)),
        ],
        compiler_params=pltpu.CompilerParams(
            collective_id=0, has_side_effects=True, vmem_limit_bytes=63 * 1024 * 1024
        ),
        cost_estimate=pl.CostEstimate(flops=7_000_000_000, bytes_accessed=8_000_000, transcendentals=4_500_000),
        name="joint_attention",
    )(*arrays)


def solution(mesh):
    placed = (
        P(("dp", "ctx", "tp"), None),
        P(("dp", "tp"), None),
        P("dp", None),
        P("dp", None),
        P(None, "tp"),
        P("ctx", "tp"),
        P("tp", None),
        P("tp", "ctx"),
        P(),
    )
    return jax.shard_map(
        on_device,
        mesh=mesh,
        in_specs=placed,
        out_specs=(P(("dp", "ctx", "tp"), None), P(("dp", "tp"), "ctx")),
        check_vma=False,
    )
```
